32 devices in a mesh: section: 4 (over x, core), tile: 8 (over z, y).
Axes of the slice: x: 2, y: 2, z: 4, core: 2. Of those that a mesh axis runs over, the one named last changes fastest.
Arguments:
- saved: float32 [4, 5, 8, 64, 128], P('section', None, None, 'tile'), may hold values from -2.5 to 2.5
- sched: int32 [4], replicated, may hold values from 0 to 3, each once
Outputs:
- gradient: float32 [5, 8, 64, 128], P(None, None, 'tile')
The draws below stay inside these ranges and needn't reach their ends.
Inputs may be any that keep to these rules, and one draw needn't show every extreme that they name: sched is a permutation of 0 .. 3.
All inputs are finite; a program needn't handle non-finite values.
Results may differ from the reference program's by a relative error of at most 0.0001.
Values sent between devices are 32-bit elements; how exact they have to be, the bound alone decides.
No kernel may reach another device: no remote copies, remote signals or barrier semaphores. Data moves between devices by JAX's collectives and lax.ppermute only.
A program may use at most 64 MiB of HBM per device.

```python
import jax
import jax.numpy as jnp
from jax import lax

NY = 128
NZ = 8
FIELDS = 5
SPAN = 1
GROUPS = 4
NX = 64


def level_of(key, extent, cuts, smallest, top_value):
    def one(dim, blocks):
        draws = jax.random.uniform(jax.random.fold_in(jax.random.fold_in(key, 6), dim), (blocks,), jnp.float32, smallest / len(cuts), top_value / len(cuts))
        return jnp.repeat(jnp.exp(draws), extent[dim] // blocks).reshape((-1,) + (1,) * (len(extent) - dim - 1))

    loudness = one(*cuts[0])
    for cut in cuts[1:]:
        loudness = loudness * one(*cut)
    return loudness


def gaussian(rng, extent, deviation, limit, cuts=(), held_as=jnp.bfloat16):
    level = level_of(rng, extent, cuts, -0.22, 0.18) if cuts else 1.0
    array = jax.random.normal(rng, extent, jnp.float32) * deviation * level
    return jnp.minimum(jnp.maximum(array, -limit), limit).astype(held_as)


def setup_inputs(seed: int = 0) -> dict:
    key_of = jax.random.split(jax.random.key(seed), 3)
    return {
        "saved": gaussian(key_of[0], (GROUPS, FIELDS, NZ, NX, NY), 0.5, 2.5, ((0, 4), (3, 8)), jnp.float32),
        "sched": jax.random.permutation(key_of[1], GROUPS).astype(jnp.int32),
    }


time_step = 0.1
buoyancy_sq = 1.0
sound_sq = 1.0
hyper_coeff = 0.1

def slope_roll(field, along):
    near_diff = jnp.roll(field, -1, along) - jnp.roll(field, 1, along)
    far_diff = jnp.roll(field, -2, along) - jnp.roll(field, 2, along)
    return (8.0 * near_diff - far_diff) / 12.0

def hyper_roll(field, along):
    outer_sum = jnp.roll(field, -2, along) + jnp.roll(field, 2, along)
    inner_sum = jnp.roll(field, -1, along) + jnp.roll(field, 1, along)
    return outer_sum - 4.0 * inner_sum + 6.0 * field

def tendency(current):
    fields = [current[which] for which in range(5)]
    vel_x, vel_y, vel_z, buoy_field, press_field = fields

    def advect(field):
        return vel_x * slope_roll(field, 1) + vel_y * slope_roll(field, 2) + vel_z * slope_roll(field, 0)

    def smooth(field):
        return hyper_roll(field, 1) + hyper_roll(field, 2) + hyper_roll(field, 0)
    tend_u = -advect(vel_x) - slope_roll(press_field, 1) - hyper_coeff * smooth(vel_x)
    tend_v = -advect(vel_y) - slope_roll(press_field, 2) - hyper_coeff * smooth(vel_y)
    tend_w = -advect(vel_z) - slope_roll(press_field, 0) + buoy_field - hyper_coeff * smooth(vel_z)
    tend_b = -advect(buoy_field) - buoyancy_sq * vel_z - hyper_coeff * smooth(buoy_field)
    diverge = slope_roll(vel_x, 1) + slope_roll(vel_y, 2) + slope_roll(vel_z, 0)
    tend_p = -sound_sq * diverge - hyper_coeff * smooth(press_field)
    return jnp.stack([tend_u, tend_v, tend_w, tend_b, tend_p])

def advance(current):
    first = current + time_step * tendency(current)
    second = 0.75 * current + 0.25 * (first + time_step * tendency(first))
    return current / 3.0 + 2.0 / 3.0 * (second + time_step * tendency(second))

def reference(saved, sched):
    slot_ids = jnp.arange(GROUPS, dtype=jnp.int32)

    def start_of(cohort):
        position = jnp.sum(jnp.where(sched == cohort, slot_ids, 0)).astype(jnp.int32)
        return lax.dynamic_index_in_dim(saved, position, 0, keepdims=False)
    base_states = []
    current = start_of(0)
    for cohort in range(GROUPS - 1):
        current = start_of(cohort)
        for moment in range(SPAN):
            base_states.append(current)
            current = advance(current)
    adjoint = current - start_of(GROUPS - 1)
    for current in reversed(base_states):
        adjoint = jax.vjp(advance, current)[1](adjoint)[0]
    return adjoint
```

```python
import functools

import jax
import jax.numpy as jnp
from jax import lax
from jax.experimental import pallas as pl
from jax.experimental.pallas import tpu as pltpu
from jax.sharding import PartitionSpec as P

time_step = 0.1
hyper_coeff = 0.1
slope_unit = time_step / 12.0
hyper_unit = time_step * hyper_coeff
BLOCK = 4
FIELDS, NZ, NY = 5, 8, 128


def roll_y(plane, ahead):
    return pltpu.roll(plane, (-ahead) % NY, 1)


def roll_z(plane, ahead):
    return pltpu.roll(plane, (-ahead) % NZ, 0)


def sum_of(terms):
    return (terms[0] + terms[1]) + terms[2]


def blocks(low, high, visit):
    @pl.loop(0, (high - low) // BLOCK)
    def _(step):
        visit(low + step * BLOCK)


def forward_rows(state, margin, reach, slopes, finish):
    def visit(first):
        seen = {}

        def at(row, field):
            if (row, field) not in seen:
                seen[row, field] = state[first + (margin + row), field]
            return seen[row, field]

        for row in range(BLOCK):
            slope, near, far = {}, {}, {}
            for field in range(FIELDS if finish else 4):
                here = at(row, field)
                around = (
                    (at(row + 1, field), at(row - 1, field), at(row + 2, field), at(row - 2, field)),
                    tuple(roll_y(here, k) for k in (1, -1, 2, -2)),
                    tuple(roll_z(here, k) for k in (1, -1, 2, -2)),
                )
                for dim, (up, down, up2, down2) in enumerate(around):
                    slope[field, dim] = 8.0 * (up - down) - (up2 - down2)
                if finish:
                    near[field] = sum_of([a[0] + a[1] for a in around])
                    far[field] = sum_of([a[2] + a[3] for a in around])
            for field in range(4):
                for dim in range(3):
                    slopes[first + (reach + row), field * 3 + dim] = slope[field, dim]
            if not finish:
                continue
            vel = [at(row, dim) * slope_unit for dim in range(3)]
            moved = []
            for field in range(FIELDS):
                value = (1.0 - 18.0 * hyper_unit) * at(row, field)
                value = value + (4.0 * hyper_unit) * near[field] - hyper_unit * far[field]
                if field < 4:
                    value = value - sum_of([vel[dim] * slope[field, dim] for dim in range(3)])
                if field < 3:
                    value = value - slope_unit * slope[4, field]
                if field == 2:
                    value = value + time_step * at(row, 3)
                if field == 3:
                    value = value - time_step * at(row, 2)
                if field == 4:
                    value = value - slope_unit * sum_of([slope[dim, dim] for dim in range(3)])
                moved.append(value)
            finish(first, row, moved)

    blocks(-reach, 8 + reach, visit)


def back_rows(adjoint, state, margin, slopes, slope_margin, reach, finish):
    def visit(first):
        seen_adjoint, seen_vel, seen_prod, seen_hyper = {}, {}, {}, {}

        def adj(row, field):
            if (row, field) not in seen_adjoint:
                seen_adjoint[row, field] = adjoint[first + (reach + 2 + row), field]
            return seen_adjoint[row, field]

        def vel(row, dim):
            if (row, dim) not in seen_vel:
                seen_vel[row, dim] = state[first + (margin + row), dim] * slope_unit
            return seen_vel[row, dim]

        def prod(row, field, dim):
            key = (row, field, dim)
            if key not in seen_prod:
                if field < 4:
                    value = vel(row, dim) * adj(row, field)
                    if field == dim:
                        value = value + slope_unit * adj(row, 4)
                else:
                    value = slope_unit * adj(row, dim)
                seen_prod[key] = value
            return seen_prod[key]

        def hyper(row, field):
            if (row, field) not in seen_hyper:
                seen_hyper[row, field] = hyper_unit * adj(row, field)
            return seen_hyper[row, field]

        for row in range(BLOCK):
            pulled = []
            for field in range(FIELDS):

                def up(r, dim):
                    return 4.0 * hyper(r, field) + 8.0 * prod(r, field, dim)

                def down(r, dim):
                    return 4.0 * hyper(r, field) - 8.0 * prod(r, field, dim)

                def up2(r, dim):
                    return prod(r, field, dim) + hyper(r, field)

                def down2(r, dim):
                    return prod(r, field, dim) - hyper(r, field)

                along_x = (up(row + 1, 0) + down(row - 1, 0)) + (down2(row - 2, 0) - up2(row + 2, 0))
                along_y = (roll_y(up(row, 1), 1) + roll_y(down(row, 1), -1)) + (
                    roll_y(down2(row, 1), -2) - roll_y(up2(row, 1), 2)
                )
                along_z = (roll_z(up(row, 2), 1) + roll_z(down(row, 2), -1)) + (
                    roll_z(down2(row, 2), -2) - roll_z(up2(row, 2), 2)
                )
                value = (1.0 - 18.0 * hyper_unit) * adj(row, field) + sum_of([along_x, along_y, along_z])
                if field < 3:
                    s = [adj(row, k) * slopes[first + (slope_margin + row), k * 3 + field] for k in range(4)]
                    value = value - slope_unit * ((s[0] + s[1]) + (s[2] + s[3]))
                if field == 2:
                    value = value - time_step * adj(row, 3)
                if field == 3:
                    value = value + time_step * adj(row, 2)
                pulled.append(value)
            finish(first, row, pulled)

    blocks(-reach, 8 + reach, visit)


def store(ref, margin, scale=None):
    def finish(first, row, values):
        for field in range(FIELDS):
            ref[first + (margin + row), field] = values[field] if scale is None else scale * values[field]

    return finish


def stages(m, q0, q1, q2, slopes):
    def second(first, row, values):
        for field in range(FIELDS):
            kept = q0[first + (q0.shape[0] // 2 - 4 + row), field]
            q2[first + (q2.shape[0] // 2 - 4 + row), field] = 0.75 * kept + 0.25 * values[field]

    reach1, reach2 = q1.shape[0] // 2 - 4, q2.shape[0] // 2 - 4
    forward_rows(q0, q0.shape[0] // 2 - 4, reach1, slopes[0], store(q1, reach1))
    forward_rows(q1, reach1, reach2, slopes[1], second)


def step_back(m, adjoint, q0, q1, q2, slopes, back2, back1, finish):
    def margin(ref):
        return ref.shape[0] // 2 - 4

    back_rows(adjoint, q2, margin(q2), slopes[2], margin(slopes[2]), m + 4, store(back2, m + 4, 2.0 / 3.0))
    back_rows(back2, q1, margin(q1), slopes[1], margin(slopes[1]), m + 2, store(back1, m + 2, 0.25))

    def last(first, row, values):
        total = []
        for field in range(FIELDS):
            held = adjoint[first + (m + 6 + row), field] * (1.0 / 3.0)
            total.append((held + 0.75 * back2[first + (m + 4 + row), field]) + values[field])
        finish(first, row, total)

    back_rows(back1, q0, margin(q0), slopes[0], margin(slopes[0]), m, last)


def slot_of(sched, group, count):
    slot = jnp.int32(0)
    for k in range(count):
        slot = jnp.where(sched[k] == group, jnp.int32(k), slot)
    return slot


def take_row(states, slot, field, row):
    return states[slot, field, pl.ds(row, NZ, stride=8), :]


def pack_body(groups, sched, core, states, near, next_near, late_near, late_next):
    q0, q1, q2, target = (slot_of(sched, g, groups) for g in (0, 1, groups - 2, groups - 1))

    def fill(ref, at, slot, rows):
        for k, row in enumerate(rows):
            for field in range(FIELDS):
                ref[at + k, field] = take_row(states, slot, field, row)

    for c in (0, 1):

        @pl.when(core[0] == c)
        def _():
            def edge(count):
                return range(count) if c == 0 else range(8 - count, 8)

            fill(near, 0, q2, range(8))
            fill(near, 8, target, edge(6))
            fill(next_near, 0, q2, edge(4))
            fill(late_near, 0, q1, range(8))
            fill(late_near, 8, q0, range(8))
            fill(late_next, 0, q1, range(8))
            fill(late_next, 8, q0, edge(2))


def put_rows(dst, at, src, begin, count):
    for k in range(count):
        for field in range(FIELDS):
            dst[at + k, field] = src[begin + k, field]


def with_sides(core, own, other, place):
    @pl.when(core[0] == 0)
    def _():
        place(other, own)

    @pl.when(core[0] != 0)
    def _():
        place(own, other)


def first_body(groups, sched, core, states, own, own2, other, other2, out, edge, q0, q1, q2, goal, last, back2, back1, s0, s1, s2):
    slot_q, slot_t = (slot_of(sched, g, groups) for g in (groups - 2, groups - 1))
    for row in range(8):
        for field in range(FIELDS):
            q0[12 + row, field] = take_row(states, slot_q, field, row)
            goal[6 + row, field] = take_row(states, slot_t, field, row)

    def place(below, above):
        (b1, b2), (a1, a2) = below, above
        put_rows(q0, 0, b2, 0, 4)
        put_rows(q0, 4, b1, 0, 8)
        put_rows(q0, 20, a1, 0, 8)
        put_rows(q0, 28, a2, 0, 4)
        put_rows(goal, 0, b1, 8, 6)
        put_rows(goal, 14, a1, 8, 6)

    with_sides(core, (own, own2), (other, other2), place)
    stages(2, q0, q1, q2, (s0, s1))

    def misfit(first, row, values):
        for field in range(FIELDS):
            state = q0[first + (12 + row), field] * (1.0 / 3.0) + (2.0 / 3.0) * values[field]
            last[first + (6 + row), field] = state - goal[first + (6 + row), field]

    forward_rows(q2, 8, 6, s2, misfit)
    step_back(0, last, q0, q1, q2, (s0, s1, s2), back2, back1, store(out, 0))
    for c in (0, 1):

        @pl.when(core[0] == c)
        def _():
            put_rows(edge, 0, out, 4 * c, 4)


def second_body(
    groups, sched, core, states, adjoint, a_own, a_own2, a_other, a_other2, l_own, l_own2, l_other, l_other2, out,
    p0, p1, p2, x0, x1, x2, lam, mid, back2, back1, ps0, ps1, ps2, xs0, xs1, xs2,
):
    slot_p, slot_x = (slot_of(sched, g, groups) for g in (1, 0))
    for row in range(8):
        for field in range(FIELDS):
            p0[16 + row, field] = take_row(states, slot_p, field, row)
            x0[10 + row, field] = take_row(states, slot_x, field, row)

    def place(below, above):
        (b1, b2), (a1, a2) = below, above
        put_rows(p0, 0, b2, 0, 8)
        put_rows(p0, 8, b1, 0, 8)
        put_rows(p0, 24, a1, 0, 8)
        put_rows(p0, 32, a2, 0, 8)
        put_rows(x0, 0, b2, 8, 2)
        put_rows(x0, 2, b1, 8, 8)
        put_rows(x0, 18, a1, 8, 8)
        put_rows(x0, 26, a2, 8, 2)

    with_sides(core, (l_own, l_own2), (l_other, l_other2), place)
    stages(6, p0, p1, p2, (ps0, ps1))
    forward_rows(p2, 12, 10, ps2, None)
    stages(0, x0, x1, x2, (xs0, xs1))
    forward_rows(x2, 6, 4, xs2, None)

    def place_adjoint(below, above):
        (b1, b2), (a1, a2) = below, above
        put_rows(lam, 0, b2, 0, 4)
        put_rows(lam, 4, b1, 0, 8)
        put_rows(lam, 20, a1, 0, 8)
        put_rows(lam, 28, a2, 0, 4)

    put_rows(lam, 12, adjoint, 0, 8)
    with_sides(core, (a_own, a_own2), (a_other, a_other2), place_adjoint)
    step_back(6, lam, p0, p1, p2, (ps0, ps1, ps2), back2, back1, store(mid, 6))

    def finish(first, row, values):
        for field in range(FIELDS):
            out[field, pl.ds(first + row, NZ, stride=8), :] = values[field]

    step_back(0, mid, x0, x1, x2, (xs0, xs1, xs2), back2, back1, finish)


def rows(count, planes=FIELDS):
    return pltpu.VMEM((count, planes, NZ, NY), jnp.float32)


def kernel(body, name, inputs, outs, scratch):
    smem, vmem = pl.BlockSpec(memory_space=pltpu.SMEM), pl.BlockSpec(memory_space=pltpu.VMEM)
    return pl.pallas_call(
        body,
        out_shape=[jax.ShapeDtypeStruct(shape, jnp.float32) for shape in outs],
        in_specs=[smem, smem] + [vmem] * inputs,
        out_specs=[vmem] * len(outs),
        scratch_shapes=scratch,
        compiler_params=pltpu.CompilerParams(vmem_limit_bytes=40 * 1024 * 1024),
        name=name,
    )


def body(saved, sched):
    sections, tiles = lax.axis_size("section"), lax.axis_size("tile")
    core = (lax.axis_index("section") % 2).astype(jnp.int32).reshape(1)

    def shift(array, hops):
        pairs = []
        for s in range(sections):
            for t in range(tiles):
                to = (t - hops if s % 2 == 0 else t + hops) % tiles
                pairs.append((s * tiles + t, s * tiles + to))
        return lax.ppermute(array, ("section", "tile"), pairs)

    def swap(array):
        return lax.ppermute(array, "section", [(s, s ^ 1) for s in range(sections)])

    def block(count):
        return (count, FIELDS, NZ, NY)

    states = lax.all_gather(saved[0], "section", axis=0, tiled=False)
    states = states.reshape(sections, FIELDS, NZ * 8, NY)
    pack = kernel(functools.partial(pack_body, sections), "pack", 1, [block(14), block(4), block(16), block(10)], [])
    near, next_near, late_near, late_next = pack(sched, core, states)
    own, own2 = shift(near, 1), shift(next_near, 2)
    other, other2 = swap(own), swap(own2)
    first = kernel(
        functools.partial(first_body, sections), "first_step", 5, [block(8), block(4)],
        [rows(32), rows(28), rows(24), rows(20), rows(20), rows(16), rows(12), rows(28, 12), rows(24, 12), rows(20, 12)],
    )
    adjoint, edge = first(sched, core, states, own, own2, other, other2)
    l_own, l_own2 = shift(late_near, 1), shift(late_next, 2)
    l_other, l_other2 = swap(l_own), swap(l_own2)
    a_own, a_own2 = shift(adjoint, 1), shift(edge, 2)
    a_other, a_other2 = swap(a_own), swap(a_own2)
    second = kernel(
        functools.partial(second_body, sections), "last_steps", 10, [(FIELDS, NZ * 8, NY)],
        [rows(40), rows(36), rows(32), rows(28), rows(24), rows(20), rows(32), rows(20), rows(28), rows(24)]
        + [rows(36, 12), rows(32, 12), rows(28, 12), rows(24, 12), rows(20, 12), rows(16, 12)],
    )
    (gradient,) = second(
        sched, core, states, adjoint, a_own, a_own2, a_other, a_other2, l_own, l_own2, l_other, l_other2
    )
    return gradient.reshape(FIELDS, NZ, 8, NY)


def solution(mesh):
    placed = (P("section", None, None, "tile", None), P())
    return jax.shard_map(
        body, mesh=mesh, in_specs=placed, out_specs=P(None, None, "tile", None), check_vma=False
    )
```

```python
import jax
import jax.numpy as jnp
from jax import lax
from jax.experimental import pallas as pl
from jax.experimental.pallas import tpu as pltpu
from jax.sharding import PartitionSpec as P

time_step = 0.1
hyper_coeff = 0.1
slope_unit = time_step / 12.0
hyper_unit = time_step * hyper_coeff
BLOCK = 4
FIELDS, NZ, NY = 5, 8, 128


def roll_y(plane, ahead):
    return pltpu.roll(plane, (-ahead) % NY, 1)


def roll_z(plane, ahead):
    return pltpu.roll(plane, (-ahead) % NZ, 0)


def sum_of(terms):
    return (terms[0] + terms[1]) + terms[2]


def blocks(low, high, visit):
    @pl.loop(0, (high - low) // BLOCK)
    def _(step):
        visit(low + step * BLOCK)


def margin(ref):
    return ref.shape[0] // 2 - 4


def forward_rows(state, slopes, finish):
    reach = margin(slopes)

    def visit(first):
        seen = {}

        def at(row, field):
            if (row, field) not in seen:
                seen[row, field] = state[first + (margin(state) + row), field]
            return seen[row, field]

        for row in range(BLOCK):
            slope, near, far = {}, {}, {}
            for field in range(FIELDS if finish else 4):
                here = at(row, field)
                around = (
                    (at(row + 1, field), at(row - 1, field), at(row + 2, field), at(row - 2, field)),
                    tuple(roll_y(here, k) for k in (1, -1, 2, -2)),
                    tuple(roll_z(here, k) for k in (1, -1, 2, -2)),
                )
                for dim, (up, down, up2, down2) in enumerate(around):
                    slope[field, dim] = 8.0 * (up - down) - (up2 - down2)
                if finish:
                    near[field] = sum_of([a[0] + a[1] for a in around])
                    far[field] = sum_of([a[2] + a[3] for a in around])
            for field in range(4):
                for dim in range(3):
                    slopes[first + (reach + row), field * 3 + dim] = slope[field, dim]
            if not finish:
                continue
            vel = [at(row, dim) * slope_unit for dim in range(3)]
            moved = []
            for field in range(FIELDS):
                value = (1.0 - 18.0 * hyper_unit) * at(row, field)
                value = value + (4.0 * hyper_unit) * near[field] - hyper_unit * far[field]
                if field < 4:
                    value = value - sum_of([vel[dim] * slope[field, dim] for dim in range(3)])
                if field < 3:
                    value = value - slope_unit * slope[4, field]
                if field == 2:
                    value = value + time_step * at(row, 3)
                if field == 3:
                    value = value - time_step * at(row, 2)
                if field == 4:
                    value = value - slope_unit * sum_of([slope[dim, dim] for dim in range(3)])
                moved.append(value)
            finish(first, row, moved)

    blocks(-reach, 8 + reach, visit)


def back_rows(adjoint, state, slopes, reach, finish):
    def visit(first):
        seen_adjoint, seen_vel, seen_prod, seen_hyper = {}, {}, {}, {}

        def adj(row, field):
            if (row, field) not in seen_adjoint:
                seen_adjoint[row, field] = adjoint[first + (margin(adjoint) + row), field]
            return seen_adjoint[row, field]

        def vel(row, dim):
            if (row, dim) not in seen_vel:
                seen_vel[row, dim] = state[first + (margin(state) + row), dim] * slope_unit
            return seen_vel[row, dim]

        def prod(row, field, dim):
            key = (row, field, dim)
            if key not in seen_prod:
                if field < 4:
                    value = vel(row, dim) * adj(row, field)
                    if field == dim:
                        value = value + slope_unit * adj(row, 4)
                else:
                    value = slope_unit * adj(row, dim)
                seen_prod[key] = value
            return seen_prod[key]

        def hyper(row, field):
            if (row, field) not in seen_hyper:
                seen_hyper[row, field] = hyper_unit * adj(row, field)
            return seen_hyper[row, field]

        for row in range(BLOCK):
            pulled = []
            for field in range(FIELDS):

                def up(r, dim):
                    return 4.0 * hyper(r, field) + 8.0 * prod(r, field, dim)

                def down(r, dim):
                    return 4.0 * hyper(r, field) - 8.0 * prod(r, field, dim)

                def up2(r, dim):
                    return prod(r, field, dim) + hyper(r, field)

                def down2(r, dim):
                    return prod(r, field, dim) - hyper(r, field)

                along_x = (up(row + 1, 0) + down(row - 1, 0)) + (down2(row - 2, 0) - up2(row + 2, 0))
                along_y = (roll_y(up(row, 1), 1) + roll_y(down(row, 1), -1)) + (
                    roll_y(down2(row, 1), -2) - roll_y(up2(row, 1), 2)
                )
                along_z = (roll_z(up(row, 2), 1) + roll_z(down(row, 2), -1)) + (
                    roll_z(down2(row, 2), -2) - roll_z(up2(row, 2), 2)
                )
                value = (1.0 - 18.0 * hyper_unit) * adj(row, field) + sum_of([along_x, along_y, along_z])
                if field < 3:
                    s = [adj(row, k) * slopes[first + (margin(slopes) + row), k * 3 + field] for k in range(4)]
                    value = value - slope_unit * ((s[0] + s[1]) + (s[2] + s[3]))
                if field == 2:
                    value = value - time_step * adj(row, 3)
                if field == 3:
                    value = value + time_step * adj(row, 2)
                pulled.append(value)
            finish(first, row, pulled)

    blocks(-reach, 8 + reach, visit)


def store(ref, scale=None):
    def finish(first, row, values):
        for field in range(FIELDS):
            ref[first + (margin(ref) + row), field] = values[field] if scale is None else scale * values[field]

    return finish


def stages(q0, q1, q2, slopes):
    def second(first, row, values):
        for field in range(FIELDS):
            kept = q0[first + (margin(q0) + row), field]
            q2[first + (margin(q2) + row), field] = 0.75 * kept + 0.25 * values[field]

    forward_rows(q0, slopes[0], store(q1))
    forward_rows(q1, slopes[1], second)


def step_back(adjoint, states, slopes, back2, back1, reach, finish):
    back_rows(adjoint, states[2], slopes[2], reach[0], store(back2, 2.0 / 3.0))
    back_rows(back2, states[1], slopes[1], reach[1], store(back1, 0.25))

    def last(first, row, values):
        total = []
        for field in range(FIELDS):
            held = adjoint[first + (margin(adjoint) + row), field] * (1.0 / 3.0)
            total.append((held + 0.75 * back2[first + (margin(back2) + row), field]) + values[field])
        finish(first, row, total)

    back_rows(back1, states[0], slopes[0], reach[2], last)


def clear_sides(ref, inner):
    count = margin(ref) - inner
    zero = jnp.zeros((NZ, NY), jnp.float32)
    for row in list(range(count)) + list(range(ref.shape[0] - count, ref.shape[0])):
        for plane in range(ref.shape[1]):
            ref[row, plane] = zero


def copy_rows(dst, at, src, begin, count):
    for k in range(count):
        for field in range(FIELDS):
            dst[at + k, field] = src[begin + k, field]


def turn(states, mask, source):
    for row in range(8):
        for field in range(FIELDS):
            states[mask, row, field] = source[field, pl.ds(row, NZ, stride=8), :]


def turn_body(sched, saved, place, rows):
    section = lax.axis_index("section")
    place[0] = section & 1
    for mask in range(4):
        place[1 + sched[section ^ mask]] = mask
    turn(rows, 0, saved)


def pack_body(place, rows, beside, across, corner, states, near, next_near, late):
    copy_rows(states.at[0], 0, rows.at[0], 0, 8)
    for mask, source in ((1, beside), (2, across), (3, corner)):
        turn(states, mask, source)
    core = place[0]
    last, goal, middle, start = (states.at[place[1 + group]] for group in (2, 3, 1, 0))
    copy_rows(near, 0, last, 0, 8)
    copy_rows(near, 8, goal, 2 * core, 6)
    copy_rows(near, 14, middle, 2 * core, 6)
    copy_rows(next_near, 0, last, 4 * core, 4)
    copy_rows(next_near, 4, start, 6 * core, 2)
    copy_rows(late, 0, start, 0, 8)


def with_sides(place, own, other, put):
    @pl.when(place[0] == 0)
    def _():
        put(other, own)

    @pl.when(place[0] != 0)
    def _():
        put(own, other)


def first_body(
    place, states, own, own2, other, other2, out, edge, next_edge,
    q0, q1, q2, goal, last, qb2, qb1, qs0, qs1, qs2, lam, p0, p1, p2, pb2, pb1, ps0, ps1, ps2,
):
    copy_rows(q0, 12, states.at[place[3]], 0, 8)
    copy_rows(goal, 6, states.at[place[4]], 0, 8)
    copy_rows(p0, 8, states.at[place[2]], 0, 8)

    def put(below, above):
        (b1, b2), (a1, a2) = below, above
        copy_rows(q0, 0, b2, 0, 4)
        copy_rows(q0, 4, b1, 0, 8)
        copy_rows(q0, 20, a1, 0, 8)
        copy_rows(q0, 28, a2, 0, 4)
        copy_rows(goal, 0, b1, 8, 6)
        copy_rows(goal, 14, a1, 8, 6)
        copy_rows(p0, 2, b1, 14, 6)
        copy_rows(p0, 16, a1, 14, 6)

    with_sides(place, (own, own2), (other, other2), put)
    for ref, inner in ((p0, 6), (p1, 4), (p2, 2), (ps0, 4), (ps1, 2), (ps2, 0), (lam, 0), (pb2, 2), (pb1, 4)):
        clear_sides(ref, inner)
    stages(q0, q1, q2, (qs0, qs1))

    def misfit(first, row, values):
        for field in range(FIELDS):
            state = q0[first + (12 + row), field] * (1.0 / 3.0) + (2.0 / 3.0) * values[field]
            last[first + (6 + row), field] = state - goal[first + (6 + row), field]

    forward_rows(q2, qs2, misfit)
    step_back(last, (q0, q1, q2), (qs0, qs1, qs2), qb2, qb1, (4, 2, 0), store(lam))
    inner = [ref.at[pl.ds(2, ref.shape[0] - 4)] for ref in (p0, p1, p2, ps0, ps1, ps2)]
    stages(*inner[:3], inner[3:5])
    forward_rows(inner[2], inner[5], None)
    step_back(lam, (p0, p1, p2), (ps0, ps1, ps2), pb2, pb1, (2, 4, 6), store(out))
    copy_rows(edge, 0, out, 8 * place[0], 12)
    copy_rows(next_edge, 0, out, 16 * place[0], 4)


def ahead_body(place, states, own, own2, other, other2, after, x0, x1, x2, xs0, xs1, xs2):
    copy_rows(x0, 10, states.at[place[1]], 0, 8)

    def put(below, above):
        (b1, b2), (a1, a2) = below, above
        copy_rows(x0, 0, b2, 4, 2)
        copy_rows(x0, 2, b1, 0, 8)
        copy_rows(x0, 18, a1, 0, 8)
        copy_rows(x0, 26, a2, 4, 2)

    with_sides(place, (own, own2), (other, other2), put)
    stages(x0, x1, x2, (xs0, xs1))
    forward_rows(x2, xs2, None)


def last_body(place, share, own, own2, other, other2, x0, x1, x2, xs0, xs1, xs2, out, lam, back2, back1):
    def put(below, above):
        (b1, b2), (a1, a2) = below, above
        for row in range(20):
            for field in range(FIELDS):
                value = share[row, field]
                if row < 12:
                    value = value + b1[row, field]
                if row < 4:
                    value = value + b2[row, field]
                if row >= 8:
                    value = value + a1[row - 8, field]
                if row >= 16:
                    value = value + a2[row - 16, field]
                lam[row, field] = value

    with_sides(place, (own, own2), (other, other2), put)

    def finish(first, row, values):
        for field in range(FIELDS):
            out[field, pl.ds(first + row, NZ, stride=8), :] = values[field]

    step_back(lam, (x0, x1, x2), (xs0, xs1, xs2), back2, back1, (4, 2, 0), finish)


def block(count, planes=FIELDS):
    return (count, planes, NZ, NY)


def kernel(body, name, arrays, outs, scratch=(), place=0, micros=1, megabytes=16):
    smem, vmem = pl.BlockSpec(memory_space=pltpu.SMEM), pl.BlockSpec(memory_space=pltpu.VMEM)
    shapes = [jax.ShapeDtypeStruct(shape, jnp.float32) for shape in outs]
    return pl.pallas_call(
        body,
        out_shape=[jax.ShapeDtypeStruct((place,), jnp.int32)] * bool(place) + shapes,
        in_specs=[smem] + [vmem] * arrays,
        out_specs=[smem] * bool(place) + [vmem] * len(outs),
        scratch_shapes=[pltpu.VMEM(shape, jnp.float32) for shape in scratch],
        compiler_params=pltpu.CompilerParams(vmem_limit_bytes=megabytes * 1024 * 1024),
        cost_estimate=pl.CostEstimate(flops=micros * 4_000_000, bytes_accessed=micros * 3_000_000, transcendentals=0),
        name=name,
    )


def body(saved, sched):
    sections, tiles = lax.axis_size("section"), lax.axis_size("tile")

    def shift(array, hops):
        pairs = []
        for s in range(sections):
            for t in range(tiles):
                to = (t - hops if s % 2 == 0 else t + hops) % tiles
                pairs.append((s * tiles + t, s * tiles + to))
        return lax.ppermute(array, ("section", "tile"), pairs)

    def swap(array, mask=1):
        return lax.ppermute(array, "section", [(s, s ^ mask) for s in range(sections)])

    mine = saved.reshape(FIELDS, NZ * 8, NY)
    across = swap(mine, 2)
    beside = swap(mine, 1)
    place, rows = kernel(turn_body, "turn", 1, [(1, *block(8))], place=5)(sched, mine)
    across, place, rows = lax.optimization_barrier((across, place, rows))
    corner = swap(across, 1)
    states, near, next_near, late = kernel(pack_body, "pack", 4, [(4, *block(8)), block(20), block(6), block(8)])(
        place, rows, beside, across, corner
    )
    own, own2 = lax.optimization_barrier((shift(near, 1), shift(next_near, 2)))
    late, own = lax.optimization_barrier((late, own))
    l_own = shift(late, 1)
    other, other2 = swap(own), swap(own2)
    share, edge, next_edge = kernel(
        first_body, "first_steps", 5, [block(20), block(12), block(4)],
        [block(32), block(28), block(24), block(20), block(20), block(16), block(12)]
        + [block(28, 12), block(24, 12), block(20, 12)]
        + [block(20), block(24), block(20), block(16), block(20), block(24)]
        + [block(20, 12), block(16, 12), block(12, 12)], micros=7,
    )(place, states, own, own2, other, other2)
    a_own, a_own2 = shift(edge, 1), shift(next_edge, 2)
    l_own, after = lax.optimization_barrier((l_own, next_edge))
    l_other = swap(l_own)
    stage = [block(28), block(24), block(20), block(24, 12), block(20, 12), block(16, 12)]
    held = kernel(ahead_body, "ahead", 6, stage, micros=2)(place, states, l_own, own2, l_other, other2, after)
    a_own, a_own2, *held = lax.optimization_barrier((a_own, a_own2, *held))
    a_other, a_other2 = swap(a_own), swap(a_own2)
    (gradient,) = kernel(
        last_body, "last_step", 11, [(FIELDS, NZ * 8, NY)], [block(20), block(16), block(12)], micros=2
    )(place, share, a_own, a_own2, a_other, a_other2, *held)
    return gradient.reshape(FIELDS, NZ, 8, NY)


def solution(mesh):
    placed = (P("section", None, None, "tile", None), P())
    return jax.shard_map(
        body, mesh=mesh, in_specs=placed, out_specs=P(None, None, "tile", None), check_vma=False
    )
```

```python
import jax
import jax.numpy as jnp
from jax import lax
from jax.experimental import pallas as pl
from jax.experimental.pallas import tpu as pltpu
from jax.sharding import PartitionSpec as P

time_step = 0.1
hyper_coeff = 0.1
slope_unit = time_step / 12.0
hyper_unit = time_step * hyper_coeff
BLOCK = 28
FIELDS, NZ, NY = 5, 8, 128


def roll_y(plane, ahead):
    return pltpu.roll(plane, (-ahead) % NY, 1)


def roll_z(plane, ahead):
    return pltpu.roll(plane, (-ahead) % NZ, 0)


def sum_of(terms):
    return (terms[0] + terms[1]) + terms[2]


def blocks(low, high, visit):
    size = max(k for k in range(1, BLOCK + 1) if (high - low) % k == 0)

    @pl.loop(0, (high - low) // size)
    def _(step):
        visit(low + step * size, size)


def margin(ref):
    return ref.shape[0] // 2 - 4


def forward_rows(state, slopes, finish):
    reach = margin(slopes)

    def visit(first, size):
        seen = {}

        def at(row, field):
            if (row, field) not in seen:
                seen[row, field] = state[first + (margin(state) + row), field]
            return seen[row, field]

        for row in range(size):
            slope, near, far = {}, {}, {}
            for field in range(FIELDS if finish else 4):
                here = at(row, field)
                around = (
                    (at(row + 1, field), at(row - 1, field), at(row + 2, field), at(row - 2, field)),
                    tuple(roll_y(here, k) for k in (1, -1, 2, -2)),
                    tuple(roll_z(here, k) for k in (1, -1, 2, -2)),
                )
                for dim, (up, down, up2, down2) in enumerate(around):
                    slope[field, dim] = 8.0 * (up - down) - (up2 - down2)
                if finish:
                    near[field] = sum_of([a[0] + a[1] for a in around])
                    far[field] = sum_of([a[2] + a[3] for a in around])
            for field in range(4):
                for dim in range(3):
                    slopes[first + (reach + row), field * 3 + dim] = slope[field, dim]
            if not finish:
                continue
            vel = [at(row, dim) * slope_unit for dim in range(3)]
            moved = []
            for field in range(FIELDS):
                value = (1.0 - 18.0 * hyper_unit) * at(row, field)
                value = value + (4.0 * hyper_unit) * near[field] - hyper_unit * far[field]
                if field < 4:
                    value = value - sum_of([vel[dim] * slope[field, dim] for dim in range(3)])
                if field < 3:
                    value = value - slope_unit * slope[4, field]
                if field == 2:
                    value = value + time_step * at(row, 3)
                if field == 3:
                    value = value - time_step * at(row, 2)
                if field == 4:
                    value = value - slope_unit * sum_of([slope[dim, dim] for dim in range(3)])
                moved.append(value)
            finish(first, row, moved)

    blocks(-reach, 8 + reach, visit)


def back_rows(adjoint, state, slopes, reach, finish):
    def visit(first, size):
        seen_adjoint, seen_vel, seen_prod, seen_hyper = {}, {}, {}, {}

        def adj(row, field):
            if (row, field) not in seen_adjoint:
                seen_adjoint[row, field] = adjoint[first + (margin(adjoint) + row), field]
            return seen_adjoint[row, field]

        def vel(row, dim):
            if (row, dim) not in seen_vel:
                seen_vel[row, dim] = state[first + (margin(state) + row), dim] * slope_unit
            return seen_vel[row, dim]

        def prod(row, field, dim):
            key = (row, field, dim)
            if key not in seen_prod:
                if field < 4:
                    value = vel(row, dim) * adj(row, field)
                    if field == dim:
                        value = value + slope_unit * adj(row, 4)
                else:
                    value = slope_unit * adj(row, dim)
                seen_prod[key] = value
            return seen_prod[key]

        def hyper(row, field):
            if (row, field) not in seen_hyper:
                seen_hyper[row, field] = hyper_unit * adj(row, field)
            return seen_hyper[row, field]

        for row in range(size):
            pulled = []
            for field in range(FIELDS):

                def up(r, dim):
                    return 4.0 * hyper(r, field) + 8.0 * prod(r, field, dim)

                def down(r, dim):
                    return 4.0 * hyper(r, field) - 8.0 * prod(r, field, dim)

                def up2(r, dim):
                    return prod(r, field, dim) + hyper(r, field)

                def down2(r, dim):
                    return prod(r, field, dim) - hyper(r, field)

                along_x = (up(row + 1, 0) + down(row - 1, 0)) + (down2(row - 2, 0) - up2(row + 2, 0))
                along_y = (roll_y(up(row, 1), 1) + roll_y(down(row, 1), -1)) + (
                    roll_y(down2(row, 1), -2) - roll_y(up2(row, 1), 2)
                )
                along_z = (roll_z(up(row, 2), 1) + roll_z(down(row, 2), -1)) + (
                    roll_z(down2(row, 2), -2) - roll_z(up2(row, 2), 2)
                )
                value = (1.0 - 18.0 * hyper_unit) * adj(row, field) + sum_of([along_x, along_y, along_z])
                if field < 3:
                    s = [adj(row, k) * slopes[first + (margin(slopes) + row), k * 3 + field] for k in range(4)]
                    value = value - slope_unit * ((s[0] + s[1]) + (s[2] + s[3]))
                if field == 2:
                    value = value - time_step * adj(row, 3)
                if field == 3:
                    value = value + time_step * adj(row, 2)
                pulled.append(value)
            finish(first, row, pulled)

    blocks(-reach, 8 + reach, visit)


def store(ref, scale=None):
    def finish(first, row, values):
        for field in range(FIELDS):
            ref[first + (margin(ref) + row), field] = values[field] if scale is None else scale * values[field]

    return finish


def stages(q0, q1, q2, slopes):
    def second(first, row, values):
        for field in range(FIELDS):
            kept = q0[first + (margin(q0) + row), field]
            q2[first + (margin(q2) + row), field] = 0.75 * kept + 0.25 * values[field]

    forward_rows(q0, slopes[0], store(q1))
    forward_rows(q1, slopes[1], second)


def step_back(adjoint, states, slopes, back2, back1, reach, finish):
    back_rows(adjoint, states[2], slopes[2], reach[0], store(back2, 2.0 / 3.0))
    back_rows(back2, states[1], slopes[1], reach[1], store(back1, 0.25))

    def last(first, row, values):
        total = []
        for field in range(FIELDS):
            held = adjoint[first + (margin(adjoint) + row), field] * (1.0 / 3.0)
            total.append((held + 0.75 * back2[first + (margin(back2) + row), field]) + values[field])
        finish(first, row, total)

    back_rows(back1, states[0], slopes[0], reach[2], last)


def clear_sides(ref, inner):
    count = margin(ref) - inner
    zero = jnp.zeros((NZ, NY), jnp.float32)
    for row in list(range(count)) + list(range(ref.shape[0] - count, ref.shape[0])):
        for plane in range(ref.shape[1]):
            ref[row, plane] = zero


def copy_rows(dst, at, src, begin, count):
    for k in range(count):
        for field in range(FIELDS):
            dst[at + k, field] = src[begin + k, field]


def turn(states, mask, source):
    for row in range(8):
        for field in range(FIELDS):
            states[mask, row, field] = source[field, pl.ds(row, NZ, stride=8), :]


def turn_body(sched, saved, place, rows):
    section = lax.axis_index("section")
    place[0] = section & 1
    for mask in range(4):
        place[1 + sched[section ^ mask]] = mask
    turn(rows, 0, saved)


def pack_body(place, rows, beside, across, corner, states, near, next_near, soon, late):
    copy_rows(states.at[0], 0, rows.at[0], 0, 8)
    for mask, source in ((1, beside), (2, across), (3, corner)):
        turn(states, mask, source)
    core = place[0]
    last, goal, middle, start = (states.at[place[1 + group]] for group in (2, 3, 1, 0))
    copy_rows(near, 0, last, 0, 8)
    copy_rows(next_near, 0, last, 4 * core, 4)
    copy_rows(next_near, 4, start, 6 * core, 2)
    copy_rows(soon, 0, goal, 2 * core, 6)
    copy_rows(soon, 6, middle, 2 * core, 6)
    copy_rows(late, 0, start, 0, 8)


def with_sides(place, own, other, put):
    @pl.when(place[0] == 0)
    def _():
        put(other, own)

    @pl.when(place[0] != 0)
    def _():
        put(own, other)


def forward_body(place, states, own, own2, other, other2, end, q0, q1, q2, qs0, qs1, qs2):
    copy_rows(q0, 12, states.at[place[3]], 0, 8)

    def put(below, above):
        (b1, b2), (a1, a2) = below, above
        copy_rows(q0, 0, b2, 0, 4)
        copy_rows(q0, 4, b1, 0, 8)
        copy_rows(q0, 20, a1, 0, 8)
        copy_rows(q0, 28, a2, 0, 4)

    with_sides(place, (own, own2), (other, other2), put)
    stages(q0, q1, q2, (qs0, qs1))

    def finish(first, row, values):
        for field in range(FIELDS):
            kept = q0[first + (12 + row), field] * (1.0 / 3.0)
            end[first + (6 + row), field] = kept + (2.0 / 3.0) * values[field]

    forward_rows(q2, qs2, finish)


def first_body(
    place, states, own, other, end, q0, q1, q2, qs0, qs1, qs2, out, edge, next_edge,
    last, qb2, qb1, lam, p0, p1, p2, pb2, pb1, ps0, ps1, ps2,
):
    copy_rows(p0, 8, states.at[place[2]], 0, 8)

    def put(below, above):
        for row in range(20):
            for field in range(FIELDS):
                if row < 6:
                    goal = below[row, field]
                elif row < 14:
                    goal = states[place[4], row - 6, field]
                else:
                    goal = above[row - 14, field]
                last[row, field] = end[row, field] - goal
        copy_rows(p0, 2, below, 6, 6)
        copy_rows(p0, 16, above, 6, 6)

    with_sides(place, own, other, put)
    for ref, inner in ((p0, 6), (p1, 4), (p2, 2), (ps0, 4), (ps1, 2), (ps2, 0), (lam, 0), (pb2, 2), (pb1, 4)):
        clear_sides(ref, inner)
    step_back(last, (q0, q1, q2), (qs0, qs1, qs2), qb2, qb1, (4, 2, 0), store(lam))
    inner = [ref.at[pl.ds(2, ref.shape[0] - 4)] for ref in (p0, p1, p2, ps0, ps1, ps2)]
    stages(*inner[:3], inner[3:5])
    forward_rows(inner[2], inner[5], None)
    step_back(lam, (p0, p1, p2), (ps0, ps1, ps2), pb2, pb1, (2, 4, 6), store(out))
    copy_rows(edge, 0, out, 8 * place[0], 12)
    copy_rows(next_edge, 0, out, 16 * place[0], 4)


def ahead_body(place, states, own, own2, other, other2, after, x0, x1, x2, xs0, xs1, xs2):
    copy_rows(x0, 10, states.at[place[1]], 0, 8)

    def put(below, above):
        (b1, b2), (a1, a2) = below, above
        copy_rows(x0, 0, b2, 4, 2)
        copy_rows(x0, 2, b1, 0, 8)
        copy_rows(x0, 18, a1, 0, 8)
        copy_rows(x0, 26, a2, 4, 2)

    with_sides(place, (own, own2), (other, other2), put)
    stages(x0, x1, x2, (xs0, xs1))
    forward_rows(x2, xs2, None)


def last_body(place, share, own, own2, other, other2, x0, x1, x2, xs0, xs1, xs2, out, lam, back2, back1):
    def put(below, above):
        (b1, b2), (a1, a2) = below, above
        for row in range(20):
            for field in range(FIELDS):
                value = share[row, field]
                if row < 12:
                    value = value + b1[row, field]
                if row < 4:
                    value = value + b2[row, field]
                if row >= 8:
                    value = value + a1[row - 8, field]
                if row >= 16:
                    value = value + a2[row - 16, field]
                lam[row, field] = value

    with_sides(place, (own, own2), (other, other2), put)

    def finish(first, row, values):
        for field in range(FIELDS):
            out[field, pl.ds(first + row, NZ, stride=8), :] = values[field]

    step_back(lam, (x0, x1, x2), (xs0, xs1, xs2), back2, back1, (4, 2, 0), finish)


def block(count, planes=FIELDS):
    return (count, planes, NZ, NY)


def kernel(body, name, arrays, outs, scratch=(), place=0, micros=1, megabytes=16):
    smem, vmem = pl.BlockSpec(memory_space=pltpu.SMEM), pl.BlockSpec(memory_space=pltpu.VMEM)
    shapes = [jax.ShapeDtypeStruct(shape, jnp.float32) for shape in outs]
    return pl.pallas_call(
        body,
        out_shape=[jax.ShapeDtypeStruct((place,), jnp.int32)] * bool(place) + shapes,
        in_specs=[smem] + [vmem] * arrays,
        out_specs=[smem] * bool(place) + [vmem] * len(outs),
        scratch_shapes=[pltpu.VMEM(shape, jnp.float32) for shape in scratch],
        compiler_params=pltpu.CompilerParams(vmem_limit_bytes=megabytes * 1024 * 1024),
        cost_estimate=pl.CostEstimate(flops=micros * 4_000_000, bytes_accessed=micros * 3_000_000, transcendentals=0),
        name=name,
    )


def body(saved, sched):
    sections, tiles = lax.axis_size("section"), lax.axis_size("tile")

    def shift(array, hops):
        pairs = []
        for s in range(sections):
            for t in range(tiles):
                to = (t - hops if s % 2 == 0 else t + hops) % tiles
                pairs.append((s * tiles + t, s * tiles + to))
        return lax.ppermute(array, ("section", "tile"), pairs)

    def swap(array, mask=1):
        return lax.ppermute(array, "section", [(s, s ^ mask) for s in range(sections)])

    mine = saved.reshape(FIELDS, NZ * 8, NY)
    across = swap(mine, 2)
    beside = swap(mine, 1)
    place, rows = kernel(turn_body, "turn", 1, [(1, *block(8))], place=5)(sched, mine)
    across, place, rows = lax.optimization_barrier((across, place, rows))
    corner = swap(across, 1)
    states, near, next_near, soon, late = kernel(
        pack_body, "pack", 4, [(4, *block(8)), block(8), block(6), block(12), block(8)]
    )(place, rows, beside, across, corner)
    own, own2 = shift(near, 1), shift(next_near, 2)
    late, own2 = lax.optimization_barrier((late, own2))
    l_own = shift(late, 1)
    s_own = shift(soon, 1)
    other, other2 = swap(own), swap(own2)
    stage = [block(32), block(28), block(24), block(28, 12), block(24, 12), block(20, 12)]
    end, *held = kernel(forward_body, "last_forward", 5, [block(20)] + stage, micros=3)(
        place, states, own, own2, other, other2
    )
    s_own, end = lax.optimization_barrier((s_own, end))
    share, edge, next_edge = kernel(
        first_body, "first_steps", 10, [block(20), block(12), block(4)],
        [block(20), block(16), block(12)]
        + [block(20), block(24), block(20), block(16), block(20), block(24)]
        + [block(20, 12), block(16, 12), block(12, 12)], micros=5,
    )(place, states, s_own, swap(s_own), end, *held)
    a_own, a_own2 = shift(edge, 1), shift(next_edge, 2)
    l_own, after = lax.optimization_barrier((l_own, next_edge))
    l_other = swap(l_own)
    stage = [block(28), block(24), block(20), block(24, 12), block(20, 12), block(16, 12)]
    held = kernel(ahead_body, "ahead", 6, stage, micros=2)(place, states, l_own, own2, l_other, other2, after)
    a_own, a_own2, *held = lax.optimization_barrier((a_own, a_own2, *held))
    a_other, a_other2 = swap(a_own), swap(a_own2)
    (gradient,) = kernel(
        last_body, "last_step", 11, [(FIELDS, NZ * 8, NY)], [block(20), block(16), block(12)], micros=2
    )(place, share, a_own, a_own2, a_other, a_other2, *held)
    return gradient.reshape(FIELDS, NZ, 8, NY)


def solution(mesh):
    placed = (P("section", None, None, "tile", None), P())
    return jax.shard_map(
        body, mesh=mesh, in_specs=placed, out_specs=P(None, None, "tile", None), check_vma=False
    )
```

```python
import jax
import jax.numpy as jnp
from jax import lax
from jax.experimental import pallas as pl
from jax.experimental.pallas import tpu as pltpu
from jax.sharding import PartitionSpec as P

time_step = 0.1
hyper_coeff = 0.1
slope_unit = time_step / 12.0
hyper_unit = time_step * hyper_coeff
BLOCK = 28
FIELDS, NZ, NY = 5, 8, 128


def roll_y(plane, ahead):
    return pltpu.roll(plane, (-ahead) % NY, 1)


def roll_z(plane, ahead):
    return pltpu.roll(plane, (-ahead) % NZ, 0)


def sum_of(terms):
    return (terms[0] + terms[1]) + terms[2]


def blocks(low, high, visit):
    size = max(k for k in range(1, BLOCK + 1) if (high - low) % k == 0)

    @pl.loop(0, (high - low) // size)
    def _(step):
        visit(low + step * size, size)


def margin(ref):
    return ref.shape[0] // 2 - 4


def forward_rows(state, slopes, finish):
    reach = margin(slopes)

    def visit(first, size):
        seen = {}

        def at(row, field):
            if (row, field) not in seen:
                seen[row, field] = state[first + (margin(state) + row), field]
            return seen[row, field]

        for row in range(size):
            slope, near, far = {}, {}, {}
            for field in range(FIELDS if finish else 4):
                here = at(row, field)
                around = (
                    (at(row + 1, field), at(row - 1, field), at(row + 2, field), at(row - 2, field)),
                    tuple(roll_y(here, k) for k in (1, -1, 2, -2)),
                    tuple(roll_z(here, k) for k in (1, -1, 2, -2)),
                )
                for dim, (up, down, up2, down2) in enumerate(around):
                    slope[field, dim] = 8.0 * (up - down) - (up2 - down2)
                if finish:
                    near[field] = sum_of([a[0] + a[1] for a in around])
                    far[field] = sum_of([a[2] + a[3] for a in around])
            for field in range(4):
                for dim in range(3):
                    slopes[first + (reach + row), field * 3 + dim] = slope[field, dim]
            if not finish:
                continue
            vel = [at(row, dim) * slope_unit for dim in range(3)]
            moved = []
            for field in range(FIELDS):
                value = (1.0 - 18.0 * hyper_unit) * at(row, field)
                value = value + (4.0 * hyper_unit) * near[field] - hyper_unit * far[field]
                if field < 4:
                    value = value - sum_of([vel[dim] * slope[field, dim] for dim in range(3)])
                if field < 3:
                    value = value - slope_unit * slope[4, field]
                if field == 2:
                    value = value + time_step * at(row, 3)
                if field == 3:
                    value = value - time_step * at(row, 2)
                if field == 4:
                    value = value - slope_unit * sum_of([slope[dim, dim] for dim in range(3)])
                moved.append(value)
            finish(first, row, moved)

    blocks(-reach, 8 + reach, visit)


def back_rows(adjoint, state, slopes, reach, finish):
    def visit(first, size):
        seen_adjoint, seen_vel, seen_prod, seen_hyper = {}, {}, {}, {}

        def adj(row, field):
            if (row, field) not in seen_adjoint:
                seen_adjoint[row, field] = adjoint[first + (margin(adjoint) + row), field]
            return seen_adjoint[row, field]

        def vel(row, dim):
            if (row, dim) not in seen_vel:
                seen_vel[row, dim] = state[first + (margin(state) + row), dim] * slope_unit
            return seen_vel[row, dim]

        def prod(row, field, dim):
            key = (row, field, dim)
            if key not in seen_prod:
                if field < 4:
                    value = vel(row, dim) * adj(row, field)
                    if field == dim:
                        value = value + slope_unit * adj(row, 4)
                else:
                    value = slope_unit * adj(row, dim)
                seen_prod[key] = value
            return seen_prod[key]

        def hyper(row, field):
            if (row, field) not in seen_hyper:
                seen_hyper[row, field] = hyper_unit * adj(row, field)
            return seen_hyper[row, field]

        for row in range(size):
            pulled = []
            for field in range(FIELDS):

                def up(r, dim):
                    return 4.0 * hyper(r, field) + 8.0 * prod(r, field, dim)

                def down(r, dim):
                    return 4.0 * hyper(r, field) - 8.0 * prod(r, field, dim)

                def up2(r, dim):
                    return prod(r, field, dim) + hyper(r, field)

                def down2(r, dim):
                    return prod(r, field, dim) - hyper(r, field)

                along_x = (up(row + 1, 0) + down(row - 1, 0)) + (down2(row - 2, 0) - up2(row + 2, 0))
                along_y = (roll_y(up(row, 1), 1) + roll_y(down(row, 1), -1)) + (
                    roll_y(down2(row, 1), -2) - roll_y(up2(row, 1), 2)
                )
                along_z = (roll_z(up(row, 2), 1) + roll_z(down(row, 2), -1)) + (
                    roll_z(down2(row, 2), -2) - roll_z(up2(row, 2), 2)
                )
                value = (1.0 - 18.0 * hyper_unit) * adj(row, field) + sum_of([along_x, along_y, along_z])
                if field < 3:
                    s = [adj(row, k) * slopes[first + (margin(slopes) + row), k * 3 + field] for k in range(4)]
                    value = value - slope_unit * ((s[0] + s[1]) + (s[2] + s[3]))
                if field == 2:
                    value = value - time_step * adj(row, 3)
                if field == 3:
                    value = value + time_step * adj(row, 2)
                pulled.append(value)
            finish(first, row, pulled)

    blocks(-reach, 8 + reach, visit)


def store(ref, scale=None):
    def finish(first, row, values):
        for field in range(FIELDS):
            ref[first + (margin(ref) + row), field] = values[field] if scale is None else scale * values[field]

    return finish


def stages(q0, q1, q2, slopes):
    def second(first, row, values):
        for field in range(FIELDS):
            kept = q0[first + (margin(q0) + row), field]
            q2[first + (margin(q2) + row), field] = 0.75 * kept + 0.25 * values[field]

    forward_rows(q0, slopes[0], store(q1))
    forward_rows(q1, slopes[1], second)


def step_back(adjoint, states, slopes, back2, back1, reach, finish):
    back_rows(adjoint, states[2], slopes[2], reach[0], store(back2, 2.0 / 3.0))
    back_rows(back2, states[1], slopes[1], reach[1], store(back1, 0.25))

    def last(first, row, values):
        total = []
        for field in range(FIELDS):
            held = adjoint[first + (margin(adjoint) + row), field] * (1.0 / 3.0)
            total.append((held + 0.75 * back2[first + (margin(back2) + row), field]) + values[field])
        finish(first, row, total)

    back_rows(back1, states[0], slopes[0], reach[2], last)


def clear_sides(ref, inner):
    count = margin(ref) - inner
    zero = jnp.zeros((NZ, NY), jnp.float32)
    for row in list(range(count)) + list(range(ref.shape[0] - count, ref.shape[0])):
        for plane in range(ref.shape[1]):
            ref[row, plane] = zero


def copy_rows(dst, at, src, begin, count):
    for k in range(count):
        for field in range(FIELDS):
            dst[at + k, field] = src[begin + k, field]


def core_index():
    return lax.axis_index("section") & 1


def turn_body(sched, saved, groups, rows):
    section = lax.axis_index("section")
    for mask in range(4):
        groups[mask] = jnp.full((NZ, NY), sched[section ^ mask], jnp.int32)
    for row in range(8):
        for field in range(FIELDS):
            rows[row, field] = saved[field, pl.ds(row, NZ, stride=8), :]


def pack_body(groups, rows, beside, across, corner, states, near, next_near, soon, late):
    held = [groups[mask] for mask in range(4)]
    is_group = [[held[mask] == group for mask in range(4)] for group in range(4)]
    for row in range(8):
        for field in range(FIELDS):
            found = [rows[row, field]]
            found += [source[field, pl.ds(row, NZ, stride=8), :] for source in (beside, across, corner)]
            for group in range(4):
                value = found[0]
                for mask in range(1, 4):
                    value = jnp.where(is_group[group][mask], found[mask], value)
                states[group, row, field] = value
    core = core_index()
    start, middle, last, goal = (states.at[group] for group in range(4))
    copy_rows(near, 0, last, 0, 8)
    copy_rows(next_near, 0, last, 4 * core, 4)
    copy_rows(next_near, 4, start, 6 * core, 2)
    copy_rows(soon, 0, goal, 2 * core, 6)
    copy_rows(soon, 6, middle, 2 * core, 6)
    copy_rows(late, 0, start, 0, 8)


def with_sides(own, other, put):
    @pl.when(core_index() == 0)
    def _():
        put(other, own)

    @pl.when(core_index() != 0)
    def _():
        put(own, other)


def forward_body(states, own, own2, other, other2, end, q0, q1, q2, qs0, qs1, qs2):
    copy_rows(q0, 12, states.at[2], 0, 8)

    def put(below, above):
        (b1, b2), (a1, a2) = below, above
        copy_rows(q0, 0, b2, 0, 4)
        copy_rows(q0, 4, b1, 0, 8)
        copy_rows(q0, 20, a1, 0, 8)
        copy_rows(q0, 28, a2, 0, 4)

    with_sides((own, own2), (other, other2), put)
    stages(q0, q1, q2, (qs0, qs1))

    def finish(first, row, values):
        for field in range(FIELDS):
            kept = q0[first + (12 + row), field] * (1.0 / 3.0)
            end[first + (6 + row), field] = kept + (2.0 / 3.0) * values[field]

    forward_rows(q2, qs2, finish)


def first_body(
    states, own, other, end, q0, q1, q2, qs0, qs1, qs2, out, edge, next_edge,
    last, qb2, qb1, lam, p0, p1, p2, pb2, pb1, ps0, ps1, ps2,
):
    copy_rows(p0, 8, states.at[1], 0, 8)

    def put(below, above):
        for row in range(20):
            for field in range(FIELDS):
                if row < 6:
                    goal = below[row, field]
                elif row < 14:
                    goal = states[3, row - 6, field]
                else:
                    goal = above[row - 14, field]
                last[row, field] = end[row, field] - goal
        copy_rows(p0, 2, below, 6, 6)
        copy_rows(p0, 16, above, 6, 6)

    with_sides(own, other, put)
    for ref, inner in ((p0, 6), (p1, 4), (p2, 2), (ps0, 4), (ps1, 2), (ps2, 0), (lam, 0), (pb2, 2), (pb1, 4)):
        clear_sides(ref, inner)
    step_back(last, (q0, q1, q2), (qs0, qs1, qs2), qb2, qb1, (4, 2, 0), store(lam))
    inner = [ref.at[pl.ds(2, ref.shape[0] - 4)] for ref in (p0, p1, p2, ps0, ps1, ps2)]
    stages(*inner[:3], inner[3:5])
    forward_rows(inner[2], inner[5], None)
    step_back(lam, (p0, p1, p2), (ps0, ps1, ps2), pb2, pb1, (2, 4, 6), store(out))
    copy_rows(edge, 0, out, 8 * core_index(), 12)
    copy_rows(next_edge, 0, out, 16 * core_index(), 4)


def ahead_body(states, own, own2, other, other2, after, x0, x1, x2, xs0, xs1, xs2):
    copy_rows(x0, 10, states.at[0], 0, 8)

    def put(below, above):
        (b1, b2), (a1, a2) = below, above
        copy_rows(x0, 0, b2, 4, 2)
        copy_rows(x0, 2, b1, 0, 8)
        copy_rows(x0, 18, a1, 0, 8)
        copy_rows(x0, 26, a2, 4, 2)

    with_sides((own, own2), (other, other2), put)
    stages(x0, x1, x2, (xs0, xs1))
    forward_rows(x2, xs2, None)


def last_body(share, own, own2, other, other2, x0, x1, x2, xs0, xs1, xs2, out, lam, back2, back1):
    def put(below, above):
        (b1, b2), (a1, a2) = below, above
        for row in range(20):
            for field in range(FIELDS):
                value = share[row, field]
                if row < 12:
                    value = value + b1[row, field]
                if row < 4:
                    value = value + b2[row, field]
                if row >= 8:
                    value = value + a1[row - 8, field]
                if row >= 16:
                    value = value + a2[row - 16, field]
                lam[row, field] = value

    with_sides((own, own2), (other, other2), put)

    def finish(first, row, values):
        for field in range(FIELDS):
            out[field, pl.ds(first + row, NZ, stride=8), :] = values[field]

    step_back(lam, (x0, x1, x2), (xs0, xs1, xs2), back2, back1, (4, 2, 0), finish)


def block(count, planes=FIELDS):
    return (count, planes, NZ, NY)


def kernel(body, name, arrays, outs, scratch=(), micros=1, megabytes=16):
    vmem = pl.BlockSpec(memory_space=pltpu.VMEM)
    return pl.pallas_call(
        body,
        out_shape=[jax.ShapeDtypeStruct(shape, jnp.float32) for shape in outs],
        in_specs=[vmem] * arrays,
        out_specs=[vmem] * len(outs),
        scratch_shapes=[pltpu.VMEM(shape, jnp.float32) for shape in scratch],
        compiler_params=pltpu.CompilerParams(vmem_limit_bytes=megabytes * 1024 * 1024),
        cost_estimate=pl.CostEstimate(flops=micros * 4_000_000, bytes_accessed=micros * 3_000_000, transcendentals=0),
        name=name,
    )


def body(saved, sched):
    sections, tiles = lax.axis_size("section"), lax.axis_size("tile")

    def shift(array, hops):
        pairs = []
        for s in range(sections):
            for t in range(tiles):
                to = (t - hops if s % 2 == 0 else t + hops) % tiles
                pairs.append((s * tiles + t, s * tiles + to))
        return lax.ppermute(array, ("section", "tile"), pairs)

    def swap(array, mask=1):
        return lax.ppermute(array, "section", [(s, s ^ mask) for s in range(sections)])

    mine = saved.reshape(FIELDS, NZ * 8, NY)
    across = swap(mine, 2)
    beside = swap(mine, 1)
    smem, vmem = pl.BlockSpec(memory_space=pltpu.SMEM), pl.BlockSpec(memory_space=pltpu.VMEM)
    groups, rows = pl.pallas_call(
        turn_body,
        out_shape=[jax.ShapeDtypeStruct((4, NZ, NY), jnp.int32), jax.ShapeDtypeStruct(block(8), jnp.float32)],
        in_specs=[smem, vmem],
        out_specs=[vmem, vmem],
        compiler_params=pltpu.CompilerParams(vmem_limit_bytes=4 * 1024 * 1024),
        name="turn",
    )(sched, mine)
    across, groups, rows = lax.optimization_barrier((across, groups, rows))
    corner = swap(across, 1)
    states, near, next_near, soon, late = kernel(
        pack_body, "pack", 5, [(4, *block(8)), block(8), block(6), block(12), block(8)]
    )(groups, rows, beside, across, corner)
    own, own2 = shift(near, 1), shift(next_near, 2)
    late, own2 = lax.optimization_barrier((late, own2))
    l_own = shift(late, 1)
    s_own = shift(soon, 1)
    other, other2 = swap(own), swap(own2)
    stage = [block(32), block(28), block(24), block(28, 12), block(24, 12), block(20, 12)]
    end, *held = kernel(forward_body, "last_forward", 5, [block(20)] + stage, micros=3)(
        states, own, own2, other, other2
    )
    s_own, end = lax.optimization_barrier((s_own, end))
    share, edge, next_edge = kernel(
        first_body, "first_steps", 10, [block(20), block(12), block(4)],
        [block(20), block(16), block(12)]
        + [block(20), block(24), block(20), block(16), block(20), block(24)]
        + [block(20, 12), block(16, 12), block(12, 12)], micros=5,
    )(states, s_own, swap(s_own), end, *held)
    a_own, a_own2 = shift(edge, 1), shift(next_edge, 2)
    l_own, after = lax.optimization_barrier((l_own, next_edge))
    l_other = swap(l_own)
    stage = [block(28), block(24), block(20), block(24, 12), block(20, 12), block(16, 12)]
    held = kernel(ahead_body, "ahead", 6, stage, micros=2)(states, l_own, own2, l_other, other2, after)
    a_own, a_own2, *held = lax.optimization_barrier((a_own, a_own2, *held))
    a_other, a_other2 = swap(a_own), swap(a_own2)
    (gradient,) = kernel(
        last_body, "last_step", 11, [(FIELDS, NZ * 8, NY)], [block(20), block(16), block(12)], micros=2
    )(share, a_own, a_own2, a_other, a_other2, *held)
    return gradient.reshape(FIELDS, NZ, 8, NY)


def solution(mesh):
    placed = (P("section", None, None, "tile", None), P())
    return jax.shard_map(
        body, mesh=mesh, in_specs=placed, out_specs=P(None, None, "tile", None), check_vma=False
    )
```

```python
import jax
import jax.numpy as jnp
from jax import lax
from jax.experimental import pallas as pl
from jax.experimental.pallas import tpu as pltpu
from jax.sharding import PartitionSpec as P

time_step = 0.1
hyper_coeff = 0.1
slope_unit = time_step / 12.0
hyper_unit = time_step * hyper_coeff
BLOCK = 28
FIELDS, NZ, NY = 5, 8, 128


def roll_y(plane, ahead):
    return pltpu.roll(plane, (-ahead) % NY, 1)


def roll_z(plane, ahead):
    return pltpu.roll(plane, (-ahead) % NZ, 0)


def sum_of(terms):
    return (terms[0] + terms[1]) + terms[2]


def blocks(first, count, visit):
    size = max(k for k in range(1, BLOCK + 1) if count % k == 0)

    @pl.loop(0, count // size)
    def _(step):
        visit(first + step * size, size)


def margin(ref):
    return ref.shape[0] // 2 - 4


def forward_rows(state, slopes, finish):
    reach = margin(slopes)

    def visit(first, size):
        seen = {}

        def at(row, field):
            if (row, field) not in seen:
                seen[row, field] = state[first + (margin(state) + row), field]
            return seen[row, field]

        for row in range(size):
            slope, near, far = {}, {}, {}
            for field in range(FIELDS if finish else 4):
                here = at(row, field)
                around = (
                    (at(row + 1, field), at(row - 1, field), at(row + 2, field), at(row - 2, field)),
                    tuple(roll_y(here, k) for k in (1, -1, 2, -2)),
                    tuple(roll_z(here, k) for k in (1, -1, 2, -2)),
                )
                for dim, (up, down, up2, down2) in enumerate(around):
                    slope[field, dim] = 8.0 * (up - down) - (up2 - down2)
                if finish:
                    near[field] = sum_of([a[0] + a[1] for a in around])
                    far[field] = sum_of([a[2] + a[3] for a in around])
            for field in range(4):
                for dim in range(3):
                    slopes[first + (reach + row), field * 3 + dim] = slope[field, dim]
            if not finish:
                continue
            vel = [at(row, dim) * slope_unit for dim in range(3)]
            moved = []
            for field in range(FIELDS):
                value = (1.0 - 18.0 * hyper_unit) * at(row, field)
                value = value + (4.0 * hyper_unit) * near[field] - hyper_unit * far[field]
                if field < 4:
                    value = value - sum_of([vel[dim] * slope[field, dim] for dim in range(3)])
                if field < 3:
                    value = value - slope_unit * slope[4, field]
                if field == 2:
                    value = value + time_step * at(row, 3)
                if field == 3:
                    value = value - time_step * at(row, 2)
                if field == 4:
                    value = value - slope_unit * sum_of([slope[dim, dim] for dim in range(3)])
                moved.append(value)
            finish(first, row, moved)

    blocks(-reach, 8 + 2 * reach, visit)


def back_rows(adjoint, state, slopes, rows, finish):
    def visit(first, size):
        seen_adjoint, seen_vel, seen_prod, seen_hyper = {}, {}, {}, {}

        def adj(row, field):
            if (row, field) not in seen_adjoint:
                seen_adjoint[row, field] = adjoint[first + (margin(adjoint) + row), field]
            return seen_adjoint[row, field]

        def vel(row, dim):
            if (row, dim) not in seen_vel:
                seen_vel[row, dim] = state[first + (margin(state) + row), dim] * slope_unit
            return seen_vel[row, dim]

        def prod(row, field, dim):
            key = (row, field, dim)
            if key not in seen_prod:
                if field < 4:
                    value = vel(row, dim) * adj(row, field)
                    if field == dim:
                        value = value + slope_unit * adj(row, 4)
                else:
                    value = slope_unit * adj(row, dim)
                seen_prod[key] = value
            return seen_prod[key]

        def hyper(row, field):
            if (row, field) not in seen_hyper:
                seen_hyper[row, field] = hyper_unit * adj(row, field)
            return seen_hyper[row, field]

        for row in range(size):
            pulled = []
            for field in range(FIELDS):

                def up(r, dim):
                    return 4.0 * hyper(r, field) + 8.0 * prod(r, field, dim)

                def down(r, dim):
                    return 4.0 * hyper(r, field) - 8.0 * prod(r, field, dim)

                def up2(r, dim):
                    return prod(r, field, dim) + hyper(r, field)

                def down2(r, dim):
                    return prod(r, field, dim) - hyper(r, field)

                along_x = (up(row + 1, 0) + down(row - 1, 0)) + (down2(row - 2, 0) - up2(row + 2, 0))
                along_y = (roll_y(up(row, 1), 1) + roll_y(down(row, 1), -1)) + (
                    roll_y(down2(row, 1), -2) - roll_y(up2(row, 1), 2)
                )
                along_z = (roll_z(up(row, 2), 1) + roll_z(down(row, 2), -1)) + (
                    roll_z(down2(row, 2), -2) - roll_z(up2(row, 2), 2)
                )
                value = (1.0 - 18.0 * hyper_unit) * adj(row, field) + sum_of([along_x, along_y, along_z])
                if field < 3:
                    s = [adj(row, k) * slopes[first + (margin(slopes) + row), k * 3 + field] for k in range(4)]
                    value = value - slope_unit * ((s[0] + s[1]) + (s[2] + s[3]))
                if field == 2:
                    value = value - time_step * adj(row, 3)
                if field == 3:
                    value = value + time_step * adj(row, 2)
                pulled.append(value)
            finish(first, row, pulled)

    blocks(*rows, visit)


def store(ref, scale=None):
    def finish(first, row, values):
        for field in range(FIELDS):
            ref[first + (margin(ref) + row), field] = values[field] if scale is None else scale * values[field]

    return finish


def stages(q0, q1, q2, slopes):
    def second(first, row, values):
        for field in range(FIELDS):
            kept = q0[first + (margin(q0) + row), field]
            q2[first + (margin(q2) + row), field] = 0.75 * kept + 0.25 * values[field]

    forward_rows(q0, slopes[0], store(q1))
    forward_rows(q1, slopes[1], second)


def third_back(adjoint, back2, back1, state, slopes, rows, finish):
    def last(first, row, values):
        total = []
        for field in range(FIELDS):
            held = adjoint[first + (margin(adjoint) + row), field] * (1.0 / 3.0)
            total.append((held + 0.75 * back2[first + (margin(back2) + row), field]) + values[field])
        finish(first, row, total)

    back_rows(back1, state, slopes, rows, last)


def step_back(adjoint, states, slopes, back2, back1, finish):
    back_rows(adjoint, states[2], slopes[2], (-4, 16), store(back2, 2.0 / 3.0))
    back_rows(back2, states[1], slopes[1], (-2, 12), store(back1, 0.25))
    third_back(adjoint, back2, back1, states[0], slopes[0], (0, 8), finish)


def clear_sides(ref, inner):
    count = margin(ref) - inner
    zero = jnp.zeros((NZ, NY), jnp.float32)
    for row in list(range(count)) + list(range(ref.shape[0] - count, ref.shape[0])):
        for plane in range(ref.shape[1]):
            ref[row, plane] = zero


def copy_rows(dst, at, src, begin, count):
    for k in range(count):
        for field in range(FIELDS):
            dst[at + k, field] = src[begin + k, field]


def core_index():
    return lax.axis_index("section") & 1


def turn_body(sched, saved, groups, rows):
    section = lax.axis_index("section")
    for mask in range(4):
        groups[mask] = jnp.full((NZ, NY), sched[section ^ mask], jnp.int32)
    for row in range(8):
        for field in range(FIELDS):
            rows[row, field] = saved[field, pl.ds(row, NZ, stride=8), :]


def pack_body(groups, rows, beside, across, corner, states, near, next_near, soon, late):
    held = [groups[mask] for mask in range(4)]
    is_group = [[held[mask] == group for mask in range(4)] for group in range(4)]
    for row in range(8):
        for field in range(FIELDS):
            found = [rows[row, field]]
            found += [source[field, pl.ds(row, NZ, stride=8), :] for source in (beside, across, corner)]
            for group in range(4):
                value = found[0]
                for mask in range(1, 4):
                    value = jnp.where(is_group[group][mask], found[mask], value)
                states[group, row, field] = value
    core = core_index()
    start, middle, last, goal = (states.at[group] for group in range(4))
    copy_rows(near, 0, last, 0, 8)
    copy_rows(next_near, 0, last, 4 * core, 4)
    copy_rows(next_near, 4, start, 6 * core, 2)
    copy_rows(soon, 0, goal, 2 * core, 6)
    copy_rows(soon, 6, middle, 2 * core, 6)
    copy_rows(late, 0, start, 0, 8)


def with_sides(own, other, put):
    @pl.when(core_index() == 0)
    def _():
        put(other, own)

    @pl.when(core_index() != 0)
    def _():
        put(own, other)


def forward_body(states, own, own2, other, other2, end, q0, q1, q2, qs0, qs1, qs2):
    copy_rows(q0, 12, states.at[2], 0, 8)

    def put(below, above):
        (b1, b2), (a1, a2) = below, above
        copy_rows(q0, 0, b2, 0, 4)
        copy_rows(q0, 4, b1, 0, 8)
        copy_rows(q0, 20, a1, 0, 8)
        copy_rows(q0, 28, a2, 0, 4)

    with_sides((own, own2), (other, other2), put)
    stages(q0, q1, q2, (qs0, qs1))

    def finish(first, row, values):
        for field in range(FIELDS):
            kept = q0[first + (12 + row), field] * (1.0 / 3.0)
            end[first + (6 + row), field] = kept + (2.0 / 3.0) * values[field]

    forward_rows(q2, qs2, finish)


def first_body(
    states, own, other, end, q0, q1, q2, qs0, qs1, qs2,
    edge, next_edge, lam, pb2, pb1, p0, p1, ps0, ps1, last, qb2, qb1, p2, ps2,
):
    core = core_index()
    copy_rows(p0, 8, states.at[1], 0, 8)

    def put(below, above):
        for row in range(20):
            for field in range(FIELDS):
                if row < 6:
                    goal = below[row, field]
                elif row < 14:
                    goal = states[3, row - 6, field]
                else:
                    goal = above[row - 14, field]
                last[row, field] = end[row, field] - goal
        copy_rows(p0, 2, below, 6, 6)
        copy_rows(p0, 16, above, 6, 6)

    with_sides(own, other, put)
    for ref, inner in ((p0, 6), (p1, 4), (p2, 2), (ps0, 4), (ps1, 2), (ps2, 0), (lam, 0), (pb2, 2), (pb1, 4)):
        clear_sides(ref, inner)
    step_back(last, (q0, q1, q2), (qs0, qs1, qs2), qb2, qb1, store(lam))
    inner = [ref.at[pl.ds(2, ref.shape[0] - 4)] for ref in (p0, p1, p2, ps0, ps1, ps2)]
    stages(*inner[:3], inner[3:5])
    forward_rows(inner[2], inner[5], None)
    back_rows(lam, p2, ps2, (-2, 12), store(pb2, 2.0 / 3.0))
    back_rows(pb2, p1, ps1, (-4 + 4 * core, 12), store(pb1, 0.25))

    def finish(first, row, values):
        for field in range(FIELDS):
            edge[first + (6 - 8 * core + row), field] = values[field]

    third_back(lam, pb2, pb1, p0, ps0, (-6 + 8 * core, 12), finish)
    copy_rows(next_edge, 0, edge, 8 * core, 4)


def rest_body(lam, pb2, pb1, p0, p1, ps0, ps1, out, back1):
    core = core_index()
    copy_rows(back1, 0, pb1, 0, 24)
    back_rows(pb2, p1, ps1, (8 - 12 * core, 4), store(back1, 0.25))

    def finish(first, row, values):
        for field in range(FIELDS):
            out[first + (-6 + 12 * core + row), field] = values[field]

    third_back(lam, pb2, back1, p0, ps0, (6 - 12 * core, 8), finish)


def ahead_body(states, own, own2, other, other2, after, x0, x1, x2, xs0, xs1, xs2):
    copy_rows(x0, 10, states.at[0], 0, 8)

    def put(below, above):
        (b1, b2), (a1, a2) = below, above
        copy_rows(x0, 0, b2, 4, 2)
        copy_rows(x0, 2, b1, 0, 8)
        copy_rows(x0, 18, a1, 0, 8)
        copy_rows(x0, 26, a2, 4, 2)

    with_sides((own, own2), (other, other2), put)
    stages(x0, x1, x2, (xs0, xs1))
    forward_rows(x2, xs2, None)


def last_body(edge, rest, own, own2, other, other2, x0, x1, x2, xs0, xs1, xs2, out, lam, back2, back1):
    def put(below, above, low, high):
        (b1, b2), (a1, a2) = below, above
        for row in range(20):
            for field in range(FIELDS):
                value = low[row, field] if row < low.shape[0] else high[row - low.shape[0], field]
                if row < 12:
                    value = value + b1[row, field]
                if row < 4:
                    value = value + b2[row, field]
                if row >= 8:
                    value = value + a1[row - 8, field]
                if row >= 16:
                    value = value + a2[row - 16, field]
                lam[row, field] = value

    @pl.when(core_index() == 0)
    def _():
        put((other, other2), (own, own2), edge, rest)

    @pl.when(core_index() != 0)
    def _():
        put((own, own2), (other, other2), rest, edge)

    def finish(first, row, values):
        for field in range(FIELDS):
            out[field, pl.ds(first + row, NZ, stride=8), :] = values[field]

    step_back(lam, (x0, x1, x2), (xs0, xs1, xs2), back2, back1, finish)


def block(count, planes=FIELDS):
    return (count, planes, NZ, NY)


def kernel(body, name, arrays, outs, scratch=(), micros=1, megabytes=16):
    vmem = pl.BlockSpec(memory_space=pltpu.VMEM)
    return pl.pallas_call(
        body,
        out_shape=[jax.ShapeDtypeStruct(shape, jnp.float32) for shape in outs],
        in_specs=[vmem] * arrays,
        out_specs=[vmem] * len(outs),
        scratch_shapes=[pltpu.VMEM(shape, jnp.float32) for shape in scratch],
        compiler_params=pltpu.CompilerParams(vmem_limit_bytes=megabytes * 1024 * 1024),
        cost_estimate=pl.CostEstimate(flops=micros * 4_000_000, bytes_accessed=micros * 3_000_000, transcendentals=0),
        name=name,
    )


def body(saved, sched):
    sections, tiles = lax.axis_size("section"), lax.axis_size("tile")

    def shift(array, hops):
        pairs = []
        for s in range(sections):
            for t in range(tiles):
                to = (t - hops if s % 2 == 0 else t + hops) % tiles
                pairs.append((s * tiles + t, s * tiles + to))
        return lax.ppermute(array, ("section", "tile"), pairs)

    def swap(array, mask=1):
        return lax.ppermute(array, "section", [(s, s ^ mask) for s in range(sections)])

    mine = saved.reshape(FIELDS, NZ * 8, NY)
    across = swap(mine, 2)
    beside = swap(mine, 1)
    smem, vmem = pl.BlockSpec(memory_space=pltpu.SMEM), pl.BlockSpec(memory_space=pltpu.VMEM)
    groups, rows = pl.pallas_call(
        turn_body,
        out_shape=[jax.ShapeDtypeStruct((4, NZ, NY), jnp.int32), jax.ShapeDtypeStruct(block(8), jnp.float32)],
        in_specs=[smem, vmem],
        out_specs=[vmem, vmem],
        compiler_params=pltpu.CompilerParams(vmem_limit_bytes=4 * 1024 * 1024),
        name="turn",
    )(sched, mine)
    across, groups, rows = lax.optimization_barrier((across, groups, rows))
    corner = swap(across, 1)
    states, near, next_near, soon, late = kernel(
        pack_body, "pack", 5, [(4, *block(8)), block(8), block(6), block(12), block(8)]
    )(groups, rows, beside, across, corner)
    own, own2 = shift(near, 1), shift(next_near, 2)
    late, own2 = lax.optimization_barrier((late, own2))
    l_own = shift(late, 1)
    s_own = shift(soon, 1)
    other, other2 = swap(own), swap(own2)
    stage = [block(32), block(28), block(24), block(28, 12), block(24, 12), block(20, 12)]
    end, *held = kernel(forward_body, "last_forward", 5, [block(20)] + stage, micros=3)(
        states, own, own2, other, other2
    )
    s_own, end = lax.optimization_barrier((s_own, end))
    edge, next_edge, *middle = kernel(
        first_body, "first_steps", 10,
        [block(12), block(4), block(20), block(20), block(24), block(24), block(20), block(20, 12), block(16, 12)],
        [block(20), block(16), block(12), block(16), block(12, 12)], micros=5,
    )(states, s_own, swap(s_own), end, *held)
    a_own, a_own2 = shift(edge, 1), shift(next_edge, 2)
    l_own, after = lax.optimization_barrier((l_own, next_edge))
    l_other = swap(l_own)
    stage = [block(28), block(24), block(20), block(24, 12), block(20, 12), block(16, 12)]
    held = kernel(ahead_body, "ahead", 6, stage, micros=2)(states, l_own, own2, l_other, other2, after)
    (rest,) = kernel(rest_body, "rest", 7, [block(8)], [block(24)])(*middle)
    a_own, a_own2, rest, *held = lax.optimization_barrier((a_own, a_own2, rest, *held))
    a_other, a_other2 = swap(a_own), swap(a_own2)
    (gradient,) = kernel(
        last_body, "last_step", 12, [(FIELDS, NZ * 8, NY)], [block(20), block(16), block(12)], micros=2
    )(edge, rest, a_own, a_own2, a_other, a_other2, *held)
    return gradient.reshape(FIELDS, NZ, 8, NY)


def solution(mesh):
    placed = (P("section", None, None, "tile", None), P())
    return jax.shard_map(
        body, mesh=mesh, in_specs=placed, out_specs=P(None, None, "tile", None), check_vma=False
    )
```

```python
import jax
import jax.numpy as jnp
from jax import lax
from jax.experimental import pallas as pl
from jax.experimental.pallas import tpu as pltpu
from jax.sharding import PartitionSpec as P

time_step = 0.1
hyper_coeff = 0.1
slope_unit = time_step / 12.0
hyper_unit = time_step * hyper_coeff
BLOCK = 28
FIELDS, NZ, NY = 5, 8, 128


def roll_y(plane, ahead):
    return pltpu.roll(plane, (-ahead) % NY, 1)


def roll_z(plane, ahead):
    return pltpu.roll(plane, (-ahead) % NZ, 0)


def sum_of(terms):
    return (terms[0] + terms[1]) + terms[2]


def blocks(first, count, visit):
    size = max(k for k in range(1, BLOCK + 1) if count % k == 0)

    @pl.loop(0, count // size)
    def _(step):
        visit(first + step * size, size)


def margin(ref):
    return ref.shape[0] // 2 - 4


def forward_rows(state, slopes, finish):
    reach = margin(slopes)

    def visit(first, size):
        seen = {}

        def at(row, field):
            if (row, field) not in seen:
                seen[row, field] = state[first + (margin(state) + row), field]
            return seen[row, field]

        for row in range(size):
            slope, near, far = {}, {}, {}
            for field in range(FIELDS if finish else 4):
                here = at(row, field)
                around = (
                    (at(row + 1, field), at(row - 1, field), at(row + 2, field), at(row - 2, field)),
                    tuple(roll_y(here, k) for k in (1, -1, 2, -2)),
                    tuple(roll_z(here, k) for k in (1, -1, 2, -2)),
                )
                for dim, (up, down, up2, down2) in enumerate(around):
                    slope[field, dim] = 8.0 * (up - down) - (up2 - down2)
                if finish:
                    near[field] = sum_of([a[0] + a[1] for a in around])
                    far[field] = sum_of([a[2] + a[3] for a in around])
            for field in range(4):
                for dim in range(3):
                    slopes[first + (reach + row), field * 3 + dim] = slope[field, dim]
            if not finish:
                continue
            vel = [at(row, dim) * slope_unit for dim in range(3)]
            moved = []
            for field in range(FIELDS):
                value = (1.0 - 18.0 * hyper_unit) * at(row, field)
                value = value + (4.0 * hyper_unit) * near[field] - hyper_unit * far[field]
                if field < 4:
                    value = value - sum_of([vel[dim] * slope[field, dim] for dim in range(3)])
                if field < 3:
                    value = value - slope_unit * slope[4, field]
                if field == 2:
                    value = value + time_step * at(row, 3)
                if field == 3:
                    value = value - time_step * at(row, 2)
                if field == 4:
                    value = value - slope_unit * sum_of([slope[dim, dim] for dim in range(3)])
                moved.append(value)
            finish(first, row, moved)

    blocks(-reach, 8 + 2 * reach, visit)


def back_rows(adjoint, state, slopes, rows, finish):
    def visit(first, size):
        seen_adjoint, seen_vel, seen_prod, seen_hyper = {}, {}, {}, {}

        def adj(row, field):
            if (row, field) not in seen_adjoint:
                seen_adjoint[row, field] = adjoint[first + (margin(adjoint) + row), field]
            return seen_adjoint[row, field]

        def vel(row, dim):
            if (row, dim) not in seen_vel:
                seen_vel[row, dim] = state[first + (margin(state) + row), dim] * slope_unit
            return seen_vel[row, dim]

        def prod(row, field, dim):
            key = (row, field, dim)
            if key not in seen_prod:
                if field < 4:
                    value = vel(row, dim) * adj(row, field)
                    if field == dim:
                        value = value + slope_unit * adj(row, 4)
                else:
                    value = slope_unit * adj(row, dim)
                seen_prod[key] = value
            return seen_prod[key]

        def hyper(row, field):
            if (row, field) not in seen_hyper:
                seen_hyper[row, field] = hyper_unit * adj(row, field)
            return seen_hyper[row, field]

        for row in range(size):
            pulled = []
            for field in range(FIELDS):

                def up(r, dim):
                    return 4.0 * hyper(r, field) + 8.0 * prod(r, field, dim)

                def down(r, dim):
                    return 4.0 * hyper(r, field) - 8.0 * prod(r, field, dim)

                def up2(r, dim):
                    return prod(r, field, dim) + hyper(r, field)

                def down2(r, dim):
                    return prod(r, field, dim) - hyper(r, field)

                along_x = (up(row + 1, 0) + down(row - 1, 0)) + (down2(row - 2, 0) - up2(row + 2, 0))
                along_y = (roll_y(up(row, 1), 1) + roll_y(down(row, 1), -1)) + (
                    roll_y(down2(row, 1), -2) - roll_y(up2(row, 1), 2)
                )
                along_z = (roll_z(up(row, 2), 1) + roll_z(down(row, 2), -1)) + (
                    roll_z(down2(row, 2), -2) - roll_z(up2(row, 2), 2)
                )
                value = (1.0 - 18.0 * hyper_unit) * adj(row, field) + sum_of([along_x, along_y, along_z])
                if field < 3:
                    s = [adj(row, k) * slopes[first + (margin(slopes) + row), k * 3 + field] for k in range(4)]
                    value = value - slope_unit * ((s[0] + s[1]) + (s[2] + s[3]))
                if field == 2:
                    value = value - time_step * adj(row, 3)
                if field == 3:
                    value = value + time_step * adj(row, 2)
                pulled.append(value)
            finish(first, row, pulled)

    blocks(*rows, visit)


def store(ref, scale=None):
    def finish(first, row, values):
        for field in range(FIELDS):
            ref[first + (margin(ref) + row), field] = values[field] if scale is None else scale * values[field]

    return finish


def stages(q0, q1, q2, slopes, fields=4):
    def second(first, row, values):
        for field in range(fields):
            kept = q0[first + (margin(q0) + row), field]
            q2[first + (margin(q2) + row), field] = 0.75 * kept + 0.25 * values[field]

    forward_rows(q0, slopes[0], store(q1))
    forward_rows(q1, slopes[1], second)


def third_back(adjoint, back2, back1, state, slopes, rows, finish):
    def last(first, row, values):
        total = []
        for field in range(FIELDS):
            held = adjoint[first + (margin(adjoint) + row), field] * (1.0 / 3.0)
            total.append((held + 0.75 * back2[first + (margin(back2) + row), field]) + values[field])
        finish(first, row, total)

    back_rows(back1, state, slopes, rows, last)


def step_back(adjoint, states, slopes, back2, back1, finish):
    back_rows(adjoint, states[2], slopes[2], (-4, 16), store(back2, 2.0 / 3.0))
    back_rows(back2, states[1], slopes[1], (-2, 12), store(back1, 0.25))
    third_back(adjoint, back2, back1, states[0], slopes[0], (0, 8), finish)


def clear_sides(ref, inner):
    count = margin(ref) - inner
    zero = jnp.zeros((NZ, NY), jnp.float32)
    for row in list(range(count)) + list(range(ref.shape[0] - count, ref.shape[0])):
        for plane in range(ref.shape[1]):
            ref[row, plane] = zero


def copy_rows(dst, at, src, begin, count):
    for k in range(count):
        for field in range(FIELDS):
            dst[at + k, field] = src[begin + k, field]


def core_index():
    return lax.axis_index("section") & 1


def turn_body(sched, saved, groups, rows):
    section = lax.axis_index("section")
    for mask in range(4):
        groups[mask] = jnp.full((NZ, NY), sched[section ^ mask], jnp.int32)
    for row in range(8):
        for field in range(FIELDS):
            rows[row, field] = saved[field, pl.ds(row, NZ, stride=8), :]


def pack_body(groups, rows, beside, across, corner, states, near, next_near, soon, late):
    held = [groups[mask] for mask in range(4)]
    is_group = [[held[mask] == group for mask in range(4)] for group in range(4)]
    for row in range(8):
        for field in range(FIELDS):
            found = [rows[row, field]]
            found += [source[field, pl.ds(row, NZ, stride=8), :] for source in (beside, across, corner)]
            for group in range(4):
                value = found[0]
                for mask in range(1, 4):
                    value = jnp.where(is_group[group][mask], found[mask], value)
                states[group, row, field] = value
    core = core_index()
    start, middle, last, goal = (states.at[group] for group in range(4))
    copy_rows(near, 0, last, 0, 8)
    copy_rows(next_near, 0, last, 4 * core, 4)
    copy_rows(next_near, 4, start, 6 * core, 2)
    copy_rows(soon, 0, goal, 2 * core, 6)
    copy_rows(soon, 6, middle, 2 * core, 6)
    copy_rows(late, 0, start, 0, 8)


def with_sides(own, other, put):
    @pl.when(core_index() == 0)
    def _():
        put(other, own)

    @pl.when(core_index() != 0)
    def _():
        put(own, other)


def forward_body(states, own, own2, other, other2, end, q0, q1, q2, qs0, qs1, qs2):
    copy_rows(q0, 12, states.at[2], 0, 8)

    def put(below, above):
        (b1, b2), (a1, a2) = below, above
        copy_rows(q0, 0, b2, 0, 4)
        copy_rows(q0, 4, b1, 0, 8)
        copy_rows(q0, 20, a1, 0, 8)
        copy_rows(q0, 28, a2, 0, 4)

    with_sides((own, own2), (other, other2), put)
    stages(q0, q1, q2, (qs0, qs1), FIELDS)

    def finish(first, row, values):
        for field in range(FIELDS):
            kept = q0[first + (12 + row), field] * (1.0 / 3.0)
            end[first + (6 + row), field] = kept + (2.0 / 3.0) * values[field]

    forward_rows(q2, qs2, finish)


def first_body(
    states, own, other, end, q0, q1, q2, qs0, qs1, qs2,
    edge, next_edge, lam, pb2, pb1, p0, p1, ps0, ps1, last, qb2, qb1, p2, ps2,
):
    core = core_index()
    copy_rows(p0, 8, states.at[1], 0, 8)

    def put(below, above):
        for row in range(20):
            for field in range(FIELDS):
                if row < 6:
                    goal = below[row, field]
                elif row < 14:
                    goal = states[3, row - 6, field]
                else:
                    goal = above[row - 14, field]
                last[row, field] = end[row, field] - goal
        copy_rows(p0, 2, below, 6, 6)
        copy_rows(p0, 16, above, 6, 6)

    with_sides(own, other, put)
    for ref, inner in ((p0, 6), (p1, 4), (p2, 2), (ps0, 4), (ps1, 2), (ps2, 0), (lam, 0), (pb2, 2), (pb1, 4)):
        clear_sides(ref, inner)
    step_back(last, (q0, q1, q2), (qs0, qs1, qs2), qb2, qb1, store(lam))
    inner = [ref.at[pl.ds(2, ref.shape[0] - 4)] for ref in (p0, p1, p2, ps0, ps1, ps2)]
    stages(*inner[:3], inner[3:5])
    forward_rows(inner[2], inner[5], None)
    back_rows(lam, p2, ps2, (-2, 12), store(pb2, 2.0 / 3.0))
    back_rows(pb2, p1, ps1, (-4 + 4 * core, 12), store(pb1, 0.25))

    def finish(first, row, values):
        for field in range(FIELDS):
            edge[first + (6 - 8 * core + row), field] = values[field]

    third_back(lam, pb2, pb1, p0, ps0, (-6 + 8 * core, 12), finish)
    copy_rows(next_edge, 0, edge, 8 * core, 4)


def rest_body(lam, pb2, pb1, p0, p1, ps0, ps1, out, back1):
    core = core_index()
    copy_rows(back1, 0, pb1, 0, 24)
    back_rows(pb2, p1, ps1, (8 - 12 * core, 4), store(back1, 0.25))

    def finish(first, row, values):
        for field in range(FIELDS):
            out[first + (-6 + 12 * core + row), field] = values[field]

    third_back(lam, pb2, back1, p0, ps0, (6 - 12 * core, 8), finish)


def ahead_body(states, own, own2, other, other2, after, x0, x1, x2, xs0, xs1, xs2):
    copy_rows(x0, 10, states.at[0], 0, 8)

    def put(below, above):
        (b1, b2), (a1, a2) = below, above
        copy_rows(x0, 0, b2, 4, 2)
        copy_rows(x0, 2, b1, 0, 8)
        copy_rows(x0, 18, a1, 0, 8)
        copy_rows(x0, 26, a2, 4, 2)

    with_sides((own, own2), (other, other2), put)
    stages(x0, x1, x2, (xs0, xs1))
    forward_rows(x2, xs2, None)


def last_body(edge, rest, own, own2, other, other2, x0, x1, x2, xs0, xs1, xs2, out, lam, back2, back1):
    def put(below, above, low, high):
        (b1, b2), (a1, a2) = below, above
        for row in range(20):
            for field in range(FIELDS):
                value = low[row, field] if row < low.shape[0] else high[row - low.shape[0], field]
                if row < 12:
                    value = value + b1[row, field]
                if row < 4:
                    value = value + b2[row, field]
                if row >= 8:
                    value = value + a1[row - 8, field]
                if row >= 16:
                    value = value + a2[row - 16, field]
                lam[row, field] = value

    @pl.when(core_index() == 0)
    def _():
        put((other, other2), (own, own2), edge, rest)

    @pl.when(core_index() != 0)
    def _():
        put((own, own2), (other, other2), rest, edge)

    def finish(first, row, values):
        for field in range(FIELDS):
            out[field, pl.ds(first + row, NZ, stride=8), :] = values[field]

    step_back(lam, (x0, x1, x2), (xs0, xs1, xs2), back2, back1, finish)


def block(count, planes=FIELDS):
    return (count, planes, NZ, NY)


def kernel(body, name, arrays, outs, scratch=(), micros=1, megabytes=16):
    vmem = pl.BlockSpec(memory_space=pltpu.VMEM)
    return pl.pallas_call(
        body,
        out_shape=[jax.ShapeDtypeStruct(shape, jnp.float32) for shape in outs],
        in_specs=[vmem] * arrays,
        out_specs=[vmem] * len(outs),
        scratch_shapes=[pltpu.VMEM(shape, jnp.float32) for shape in scratch],
        compiler_params=pltpu.CompilerParams(vmem_limit_bytes=megabytes * 1024 * 1024),
        cost_estimate=pl.CostEstimate(flops=micros * 4_000_000, bytes_accessed=micros * 3_000_000, transcendentals=0),
        name=name,
    )


def body(saved, sched):
    sections, tiles = lax.axis_size("section"), lax.axis_size("tile")

    def shift(array, hops):
        pairs = []
        for s in range(sections):
            for t in range(tiles):
                to = (t - hops if s % 2 == 0 else t + hops) % tiles
                pairs.append((s * tiles + t, s * tiles + to))
        return lax.ppermute(array, ("section", "tile"), pairs)

    def swap(array, mask=1):
        return lax.ppermute(array, "section", [(s, s ^ mask) for s in range(sections)])

    mine = saved.reshape(FIELDS, NZ * 8, NY)
    across = swap(mine, 2)
    beside = swap(mine, 1)
    smem, vmem = pl.BlockSpec(memory_space=pltpu.SMEM), pl.BlockSpec(memory_space=pltpu.VMEM)
    groups, rows = pl.pallas_call(
        turn_body,
        out_shape=[jax.ShapeDtypeStruct((4, NZ, NY), jnp.int32), jax.ShapeDtypeStruct(block(8), jnp.float32)],
        in_specs=[smem, vmem],
        out_specs=[vmem, vmem],
        compiler_params=pltpu.CompilerParams(vmem_limit_bytes=4 * 1024 * 1024),
        name="turn",
    )(sched, mine)
    across, groups, rows = lax.optimization_barrier((across, groups, rows))
    corner = swap(across, 1)
    states, near, next_near, soon, late = kernel(
        pack_body, "pack", 5, [(4, *block(8)), block(8), block(6), block(12), block(8)]
    )(groups, rows, beside, across, corner)
    own, own2 = shift(near, 1), shift(next_near, 2)
    late, own2 = lax.optimization_barrier((late, own2))
    l_own = shift(late, 1)
    s_own = shift(soon, 1)
    other, other2 = swap(own), swap(own2)
    stage = [block(32), block(28), block(24), block(28, 12), block(24, 12), block(20, 12)]
    end, *held = kernel(forward_body, "last_forward", 5, [block(20)] + stage, micros=3)(
        states, own, own2, other, other2
    )
    s_own, end = lax.optimization_barrier((s_own, end))
    edge, next_edge, *middle = kernel(
        first_body, "first_steps", 10,
        [block(12), block(4), block(20), block(20), block(24), block(24), block(20), block(20, 12), block(16, 12)],
        [block(20), block(16), block(12), block(16), block(12, 12)], micros=5,
    )(states, s_own, swap(s_own), end, *held)
    a_own, a_own2 = shift(edge, 1), shift(next_edge, 2)
    l_own, after = lax.optimization_barrier((l_own, next_edge))
    l_other = swap(l_own)
    stage = [block(28), block(24), block(20), block(24, 12), block(20, 12), block(16, 12)]
    held = kernel(ahead_body, "ahead", 6, stage, micros=2)(states, l_own, own2, l_other, other2, after)
    (rest,) = kernel(rest_body, "rest", 7, [block(8)], [block(24)])(*middle)
    a_own, a_own2, rest, *held = lax.optimization_barrier((a_own, a_own2, rest, *held))
    a_other, a_other2 = swap(a_own), swap(a_own2)
    (gradient,) = kernel(
        last_body, "last_step", 12, [(FIELDS, NZ * 8, NY)], [block(20), block(16), block(12)], micros=2
    )(edge, rest, a_own, a_own2, a_other, a_other2, *held)
    return gradient.reshape(FIELDS, NZ, 8, NY)


def solution(mesh):
    placed = (P("section", None, None, "tile", None), P())
    return jax.shard_map(
        body, mesh=mesh, in_specs=placed, out_specs=P(None, None, "tile", None), check_vma=False
    )
```
